256 devices in a mesh: tm: 32 (over y, z_hi, x), space: 8 (over z_lo, core).
Axes of the slice: x: 4, y: 4, z: 8 (z_hi: 2, z_lo: 4; z = z_hi * 4 + z_lo), core: 2. Of those that a mesh axis runs over, the one named last changes fastest.
Arguments:
- features: bfloat16 [32, 64, 64, 256], P('tm', 'space'), may hold values from -6 to 6
- masks: int32 [32, 64, 64], P('tm', 'space'), may hold values from 0 to 1
- w_pix: bfloat16 [256, 256], replicated, may hold values from -0.375 to 0.375
- mask_embed: bfloat16 [256], replicated, may hold values from -4 to 4
- w_conv: bfloat16 [3, 3, 256, 256], replicated, may hold values from -0.125 to 0.125
- w_out: bfloat16 [256, 64], replicated, may hold values from -0.375 to 0.375
- w_ptr: bfloat16 [256, 256], replicated, may hold values from -0.375 to 0.375
- w_query: bfloat16 [256, 256], replicated, may hold values from -1 to 1
- w_key: bfloat16 [64, 256], replicated, may hold values from -0.75 to 0.75
- w_value: bfloat16 [64, 256], replicated, may hold values from -0.75 to 0.75
- w_proj: bfloat16 [256, 256], replicated, may hold values from -0.375 to 0.375
- mem_tpos: bfloat16 [3, 64], replicated, may hold values from -120 to 120
- ptr_tpos: bfloat16 [16, 256], replicated, may hold values from -4 to 4
- empty_memory: bfloat16 [64], replicated, may hold values from -4 to 4
Outputs:
- attended: bfloat16 [32, 64, 64, 256], P('tm', 'space')
- memory: bfloat16 [32, 64, 4096], P('tm', 'space')
- pointers: bfloat16 [32, 256], P('tm')
The draws below stay inside these ranges and needn't reach their ends.
All inputs are finite; a program needn't handle non-finite values.
Results may differ from the reference program's by a relative error of at most 0.015.
The reference program's roundings to bfloat16 on the way count: a program that leaves them out, or rounds other values in their place, can miss the bound.
Values may be sent and summed in bfloat16 or wider, within the bound.
No kernel may reach another device: no remote copies, remote signals or barrier semaphores. Data moves between devices by JAX's collectives and lax.ppermute only.
A program may use at most 128 MiB of HBM per device.

```python
import jax
import jax.numpy as jnp
from jax import lax

D = 256
MEM_DIM = 64
MEMS = 3
POINTERS = 16
GRID = 64
FRAMES = 32


def draw_masks(key, part):
    first_key, second_key = jax.random.split(key)
    density = jax.random.randint(first_key, (FRAMES, 1, 1), 16, 81)
    row_index = jnp.arange(GRID, dtype=jnp.int32).reshape(1, GRID, 1)
    threshold = density * (GRID + 2 * row_index) // GRID
    cell_draws = jax.random.randint(second_key, (FRAMES, GRID, GRID), 0, 256)
    return (cell_draws < threshold).astype(jnp.int32)


def draw_mem_tpos(key, part):
    drawn = jnp.clip(jax.random.normal(key, (MEMS, MEM_DIM), jnp.float32), -4.0, 4.0)
    return drawn.astype(jnp.bfloat16)


def steps_of(rng, shape, cuts, smallest, largest):
    def one(position, shards_of):
        draws = jax.random.uniform(jax.random.fold_in(jax.random.fold_in(rng, 6), position), (shards_of,), jnp.float32, smallest / len(cuts), largest / len(cuts))
        return jnp.repeat(jnp.exp(draws), shape[position] // shards_of).reshape((-1,) + (1,) * (len(shape) - position - 1))

    loudness = one(*cuts[0])
    for cut in cuts[1:]:
        loudness = loudness * one(*cut)
    return loudness


def bell_draw(rng, dims, scale, bound, cuts=(), kind=jnp.bfloat16):
    result = jax.random.normal(rng, dims, jnp.float32) * scale
    if len(cuts) > 0:
        result = steps_of(rng, dims, cuts, -0.22, 0.18) * result
    return jnp.clip(result, min=-bound, max=bound).astype(kind)


def setup_inputs(seed: int = 0) -> dict:
    keys = jax.random.split(jax.random.key(seed), 15)
    features = bell_draw(keys[0], (FRAMES, GRID, GRID, D), 1.0, 6.0, ((0, 32), (1, 8)))
    masks = draw_masks(jax.random.fold_in(keys[14], 71), 0)
    w_pix = bell_draw(keys[2], (D, D), D ** -0.5, 0.375)
    mask_embed = bell_draw(keys[3], (D,), 1.0, 4.0)
    w_conv = bell_draw(keys[4], (3, 3, D, D), (9 * D) ** -0.5, 0.125)
    w_out = bell_draw(keys[5], (D, MEM_DIM), D ** -0.5, 0.375)
    w_ptr = bell_draw(keys[6], (D, D), D ** -0.5, 0.375)
    w_query = bell_draw(keys[7], (D, D), (D // 9) ** -0.5, 1.0)
    w_key = bell_draw(keys[8], (MEM_DIM, D), MEM_DIM ** -0.5, 0.75)
    w_value = bell_draw(keys[9], (MEM_DIM, D), MEM_DIM ** -0.5, 0.75)
    w_proj = bell_draw(keys[10], (D, D), D ** -0.5, 0.375)
    mem_tpos = draw_mem_tpos(jax.random.fold_in(keys[14], 71), 0)
    ptr_tpos = bell_draw(keys[12], (POINTERS, D), 1.0, 4.0)
    empty_memory = bell_draw(keys[13], (MEM_DIM,), 1.0, 4.0)
    return {"features": features, "masks": masks, "w_pix": w_pix, "mask_embed": mask_embed, "w_conv": w_conv, "w_out": w_out, "w_ptr": w_ptr, "w_query": w_query, "w_key": w_key, "w_value": w_value, "w_proj": w_proj, "mem_tpos": mem_tpos, "ptr_tpos": ptr_tpos, "empty_memory": empty_memory}


def reference(features, masks, w_pix, mask_embed, w_conv, w_out, w_ptr, w_query, w_key, w_value, w_proj, mem_tpos, ptr_tpos, empty_memory):
    ptr_tok = D // MEM_DIM
    tokens = GRID * GRID
    flat_rows = features.reshape(FRAMES * tokens, D)
    mask_rows = masks.reshape(FRAMES * tokens, 1).astype(jnp.float32)
    joined_map = (jnp.dot(flat_rows, w_pix, preferred_element_type=jnp.float32) + mask_rows * mask_embed.astype(jnp.float32)).astype(jnp.bfloat16)
    joined_map = joined_map.reshape(FRAMES, GRID, GRID, D)
    padded = jnp.pad(joined_map, ((0, 0), (1, 1), (1, 1), (0, 0)))
    conv_sum = jnp.zeros((FRAMES * tokens, D), jnp.float32)
    for row_tap in range(3):
        for col_tap in range(3):
            window_rows = padded[:, row_tap:row_tap + GRID, col_tap:col_tap + GRID, :].reshape(-1, D)
            conv_sum = conv_sum + jnp.dot(window_rows, w_conv[row_tap, col_tap], preferred_element_type=jnp.float32)
    hidden = jax.nn.gelu(conv_sum, approximate=True).astype(jnp.bfloat16)
    memory = jnp.dot(hidden, w_out, preferred_element_type=jnp.float32).astype(jnp.bfloat16)
    memory = memory.reshape(FRAMES, GRID, GRID * MEM_DIM)
    pooled = jnp.einsum('ft,ftd->fd', masks.reshape(FRAMES, tokens).astype(jnp.float32), features.reshape(FRAMES, tokens, D).astype(jnp.float32))
    normed = (pooled * lax.rsqrt(lax.optimization_barrier(jnp.mean(pooled * pooled, axis=1, keepdims=True)) + 1e-06)).astype(jnp.bfloat16)
    pointers = jnp.dot(normed, w_ptr, preferred_element_type=jnp.float32).astype(jnp.bfloat16)
    mem_tokens = memory.reshape(FRAMES * tokens, MEM_DIM)
    key_base = jnp.dot(mem_tokens, w_key, preferred_element_type=jnp.float32).reshape(FRAMES, tokens, D)
    all_values = jnp.dot(mem_tokens, w_value, preferred_element_type=jnp.float32).astype(jnp.bfloat16).reshape(FRAMES, tokens, D)
    tpos_keys = jnp.dot(mem_tpos, w_key, preferred_element_type=jnp.float32)
    ptr_tpos_keys = jnp.dot(ptr_tpos[::-1].reshape(POINTERS * ptr_tok, MEM_DIM), w_key, preferred_element_type=jnp.float32)
    null_key = jnp.dot(empty_memory.reshape(1, MEM_DIM), w_key, preferred_element_type=jnp.float32).astype(jnp.bfloat16)
    null_value = jnp.dot(empty_memory.reshape(1, MEM_DIM), w_value, preferred_element_type=jnp.float32).astype(jnp.bfloat16)
    padded_ptr = jnp.concatenate([jnp.zeros((POINTERS, D), jnp.bfloat16), pointers], axis=0)
    ptr_offsets = jnp.repeat(jnp.arange(POINTERS, dtype=jnp.int32) - POINTERS, ptr_tok)
    features_f = features.reshape(FRAMES, tokens, D).astype(jnp.float32)
    centred = features_f - lax.optimization_barrier(jnp.mean(features_f, axis=2, keepdims=True))
    query_in = (centred * lax.rsqrt(lax.optimization_barrier(jnp.mean(centred * centred, axis=2, keepdims=True)) + 1e-05)).astype(jnp.bfloat16)
    queries_all = (jnp.dot(query_in.reshape(-1, D), w_query, preferred_element_type=jnp.float32) * D ** (-0.5)).astype(jnp.bfloat16)
    queries_all = queries_all.reshape(FRAMES, tokens, D)

    def attend_frame(frame):
        key_list = []
        value_list = []
        valid_list = []
        for distance in range(1, MEMS + 1):
            source = jnp.maximum(frame - distance, 0).astype(jnp.int32)
            key_list.append((key_base[source] + tpos_keys[distance - 1]).astype(jnp.bfloat16))
            value_list.append(all_values[source])
            valid_list.append(jnp.broadcast_to(frame - distance >= 0, (tokens,)))
        window = lax.dynamic_slice_in_dim(padded_ptr, frame.astype(jnp.int32), POINTERS, 0)
        ptr_tokens = window.reshape(POINTERS * ptr_tok, MEM_DIM)
        key_list.append((jnp.dot(ptr_tokens, w_key, preferred_element_type=jnp.float32) + ptr_tpos_keys).astype(jnp.bfloat16))
        value_list.append(jnp.dot(ptr_tokens, w_value, preferred_element_type=jnp.float32).astype(jnp.bfloat16))
        valid_list.append(frame + ptr_offsets >= 0)
        key_list.append(null_key)
        value_list.append(null_value)
        valid_list.append(jnp.ones((1,), bool))
        key_rows = jnp.concatenate(key_list, axis=0)
        value_rows = jnp.concatenate(value_list, axis=0)
        is_valid = jnp.concatenate(valid_list, axis=0)
        scores = lax.dot_general(queries_all[frame], key_rows, (((1,), (1,)), ((), ())), preferred_element_type=jnp.float32)
        scores = jnp.where(is_valid[None, :], scores, -jnp.inf)
        row_top = lax.optimization_barrier(jnp.max(scores, axis=1, keepdims=True))
        expo = jnp.exp(scores - row_top)
        weights = (expo / lax.optimization_barrier(jnp.sum(expo, axis=1, keepdims=True))).astype(jnp.bfloat16)
        mixed_rows = jnp.dot(weights, value_rows, preferred_element_type=jnp.float32).astype(jnp.bfloat16)
        return (features_f[frame] + jnp.dot(mixed_rows, w_proj, preferred_element_type=jnp.float32)).astype(jnp.bfloat16)
    attended = lax.map(attend_frame, jnp.arange(FRAMES, dtype=jnp.int32)).reshape(FRAMES, GRID, GRID, D)
    return (attended, memory, pointers)
```

```python
import functools

import jax
import jax.numpy as jnp
from jax import lax
from jax.experimental import pallas as pl
from jax.experimental.pallas import tpu as pltpu
from jax.sharding import PartitionSpec as P

MEMS = 3
POINTERS = 16
FRAMES = 32
BANDS = 8
ROWS = 8
COLS = 64
TOK = ROWS * COLS
HALF = TOK // 2
D = 256
MEM = 64
PAY = MEMS * HALF + 16
BOTH = ("tm", "space")
bf16 = jnp.bfloat16
f32 = jnp.float32
NT = (((1,), (1,)), ((), ()))


def call(kernel, out_shape, *args, scratch=(), in_specs=None, aliases=None, flops=0, name=None):
    vmem = pl.BlockSpec(memory_space=pltpu.VMEM)
    return pl.pallas_call(
        kernel,
        out_shape=out_shape,
        in_specs=[vmem] * len(args) if in_specs is None else in_specs,
        out_specs=jax.tree.map(lambda _: vmem, out_shape),
        scratch_shapes=list(scratch),
        input_output_aliases=aliases or {},
        compiler_params=pltpu.CompilerParams(vmem_limit_bytes=48 << 20),
        cost_estimate=pl.CostEstimate(flops=flops, bytes_accessed=1 << 20, transcendentals=0),
        name=name,
    )(*args)


def sds(shape, dtype):
    return jax.ShapeDtypeStruct(shape, dtype)


def joined_kernel(feat, mask, w_pix, embed, joined, top, bottom, pooled):
    columns = mask[...].astype(f32).T
    row = embed[...].astype(f32)
    total = jnp.zeros((8, D), f32)
    for r in range(ROWS):
        rows = feat[r * COLS : (r + 1) * COLS, :]
        column = columns[:, r : r + 1]
        value = jnp.dot(rows, w_pix[...], preferred_element_type=f32) + column * row
        value = value.astype(bf16)
        joined[r * COLS : (r + 1) * COLS, :] = value
        if r == 0:
            top[...] = value
        if r == ROWS - 1:
            bottom[...] = value
        picked = rows.astype(f32) * column
        for k in range(COLS // 8):
            total = total + picked[k * 8 : (k + 1) * 8, :]
    pooled[...] = jnp.sum(total, axis=0, keepdims=True)


def query_kernel(feat, w_query, query):
    for r in range(0, TOK, 128):
        x = feat[r : r + 128, :].astype(f32)
        x = x - jnp.mean(x, axis=1, keepdims=True)
        x = x * lax.rsqrt(jnp.mean(x * x, axis=1, keepdims=True) + 1e-05)
        y = jnp.dot(x.astype(bf16), w_query[...], preferred_element_type=f32)
        query[r : r + 128, :] = (y * D ** (-0.5)).astype(bf16)


def conv_kernel(joined, above, below, w_conv, w_out, memory, pairs, wide, tokens):
    side = lax.broadcasted_iota(jnp.int32, (COLS, D), 0)
    for r in range(ROWS + 2):
        if r == 0:
            row = above[...]
        elif r == ROWS + 1:
            row = below[...]
        else:
            row = joined[(r - 1) * COLS : r * COLS, :]
        value = row.astype(f32)
        left = jnp.where(side == 0, 0.0, pltpu.roll(value, 1, 0))
        right = jnp.where(side == COLS - 1, 0.0, pltpu.roll(value, COLS - 1, 0))
        here = slice(r * COLS, (r + 1) * COLS)
        wide[here, 0:D] = left.astype(bf16)
        wide[here, D : 2 * D] = row
        wide[here, 2 * D : 3 * D] = right.astype(bf16)
    w_twice = jnp.concatenate([w_out[...], w_out[...]], axis=1)
    for part in range(4):
        start = part * 2 * COLS
        total = None
        for a in range(3):
            window = wide[start + a * COLS : start + a * COLS + 2 * COLS, :]
            term = jnp.dot(window, w_conv[a], preferred_element_type=f32)
            total = term if total is None else total + term
        hidden = 0.5 * total * (
            1.0 + jnp.tanh(0.7978845608028654 * (total + 0.044715 * (total * total * total)))
        )
        tokens[start : start + 2 * COLS, :] = jnp.dot(
            hidden.astype(bf16), w_twice, preferred_element_type=f32
        )
    lane = lax.broadcasted_iota(jnp.int32, (8, 128), 1)
    for k in range(COLS // 2):
        even = tokens[pl.ds(2 * k, ROWS, stride=COLS), :]
        odd = tokens[pl.ds(2 * k + 1, ROWS, stride=COLS), :]
        memory[:, k * 128 : (k + 1) * 128] = jnp.where(lane < MEM, even, odd).astype(bf16)
    lane = lax.broadcasted_iota(jnp.int32, (HALF, 128), 1)
    pairs[...] = jnp.where(lane < MEM, tokens[0:HALF, :], tokens[HALF:TOK, :]).astype(bf16)


def pointer_kernel(mine, other, w_ptr, pointer):
    pooled = mine[...] + other[...]
    scale = lax.rsqrt(jnp.mean(pooled * pooled, axis=1, keepdims=True) + 1e-06)
    normed = jnp.broadcast_to(pooled * scale, (8, D)).astype(bf16)
    y = jnp.dot(normed, w_ptr[...], preferred_element_type=f32)
    pointer[...] = y[0:1, :].astype(bf16)


def payload_kernel(first, second, third, near, far, out):
    out[0:HALF, :] = first[...]
    out[HALF : 2 * HALF, :] = second[...]
    out[2 * HALF : 3 * HALF, :] = third[...]
    row = lax.broadcasted_iota(jnp.int32, (16, 128), 0)
    tail = jnp.zeros((16, 128), f32)
    a = near[...].astype(f32)
    b = far[...].astype(f32)
    for i, piece in enumerate((a[:, 0:128], a[:, 128:256], b[:, 0:128], b[:, 128:256])):
        tail = jnp.where(row == i, piece, tail)
    out[3 * HALF : 3 * HALF + 16, :] = tail.astype(bf16)


def twice(w):
    zero = jnp.zeros_like(w)
    return jnp.concatenate(
        [jnp.concatenate([w, zero], axis=1), jnp.concatenate([zero, w], axis=1)], axis=0
    )


QT = 256
CHUNK = 2 * HALF


def attention_kernel(count, first, last, *refs):
    refs = list(refs)
    place, query, w_key, w_value, mem_tpos, empty = refs[:6]
    refs = refs[6:]
    blocks, refs = refs[:count], refs[count:]
    if first:
        state_in = None
    else:
        state_in, refs = refs[:4], refs[4:]
    if last:
        feat, w_proj, ptr_tpos, attended, keys, values, top, norm, mixed, ptr_tok = refs
    else:
        top, norm, mixed, ptr_tok, keys, values = refs
    frame = place[0]
    wk = twice(w_key[...])
    wv = twice(w_value[...])
    padded = jnp.concatenate([mem_tpos[...], jnp.zeros((8 - MEMS, MEM), bf16)], axis=0)
    tpos_keys = jnp.dot(padded, w_key[...], preferred_element_type=f32)
    if first:
        token = jnp.broadcast_to(empty[...], (8, MEM))
        null_key = jnp.dot(token, w_key[...], preferred_element_type=f32).astype(bf16)
        null_value = jnp.dot(token, w_value[...], preferred_element_type=f32).astype(bf16)
        score = jnp.sum(
            query[...].astype(f32) * null_key[0:1, :].astype(f32), axis=1, keepdims=True
        )
        top[...] = score
        norm[...] = jnp.ones_like(score)
        mixed[...] = jnp.broadcast_to(null_value[0:1, :].astype(f32), (TOK, D))
    else:
        for source, target in zip(state_in, (top, norm, mixed, ptr_tok)):
            target[...] = source[...]
    for b, block in enumerate(blocks):
        tail = block[MEMS * HALF : MEMS * HALF + 16, :].astype(f32)
        ptr_tok[pl.ds(pl.multiple_of(place[1 + b] * 8, 8), 8), :] = tail[0:8, :]

    def update(rows, scores, value_rows):
        old = top[rows, :]
        new = jnp.maximum(old, jnp.max(scores, axis=1, keepdims=True))
        weights = jnp.exp(scores - new)
        fade = jnp.exp(old - new)
        norm[rows, :] = norm[rows, :] * fade + jnp.sum(weights, axis=1, keepdims=True)
        mixed[rows, :] = mixed[rows, :] * fade + jnp.dot(
            weights.astype(bf16), value_rows, preferred_element_type=f32
        )
        top[rows, :] = new

    for d in range(MEMS):

        @pl.when(frame >= d + 1)
        def _(d=d):
            shift = tpos_keys[d : d + 1, :]
            for b, block in enumerate(blocks):
                x = block[d * HALF : (d + 1) * HALF, :]
                base = b * TOK
                k = jnp.dot(x, wk, preferred_element_type=f32)
                v = jnp.dot(x, wv, preferred_element_type=f32).astype(bf16)
                keys[base : base + HALF, :] = (k[:, :D] + shift).astype(bf16)
                keys[base + HALF : base + TOK, :] = (k[:, D:] + shift).astype(bf16)
                values[base : base + HALF, :] = v[:, :D]
                values[base + HALF : base + TOK, :] = v[:, D:]
            tiles = [slice(q * QT, (q + 1) * QT) for q in range(TOK // QT)]
            found = [
                lax.dot_general(query[rows, :], keys[...], NT, preferred_element_type=f32)
                for rows in tiles
            ]
            for rows, scores in zip(tiles, found):
                update(rows, scores, values[...])

    if last:
        widened = jnp.dot(ptr_tpos[...], wk, preferred_element_type=f32)
        lane = lax.broadcasted_iota(jnp.int32, (1, POINTERS * 2), 1)
        tok = jnp.concatenate(
            [ptr_tok[s * 8 : s * 8 + 4, :] for s in range(BANDS)], axis=0
        ).astype(bf16)
        k = (jnp.dot(tok, wk, preferred_element_type=f32) + widened).astype(bf16)
        v = jnp.dot(tok, wv, preferred_element_type=f32).astype(bf16)
        valid = frame >= lane // 2 + 1
        for half in range(2):
            k_half = k[:, half * D : (half + 1) * D]
            v_half = v[:, half * D : (half + 1) * D]
            for q in range(TOK // QT):
                rows = slice(q * QT, (q + 1) * QT)
                scores = lax.dot_general(query[rows, :], k_half, NT, preferred_element_type=f32)
                update(rows, jnp.where(valid, scores, -jnp.inf), v_half)
        for q in range(TOK // QT):
            rows = slice(q * QT, (q + 1) * QT)
            final = (mixed[rows, :] / norm[rows, :]).astype(bf16)
            attended[rows, :] = (
                feat[rows, :].astype(f32)
                + jnp.dot(final, w_proj[...], preferred_element_type=f32)
            ).astype(bf16)


def attend(place, query, weights, blocks, state=None, final=None):
    smem = pl.BlockSpec(memory_space=pltpu.SMEM)
    vmem = pl.BlockSpec(memory_space=pltpu.VMEM)
    args = [place, query, *weights, *blocks]
    specs = [smem] + [vmem] * (len(args) - 1)
    if state is not None:
        args += list(state)
        specs += [vmem] * 4
    state_shape = [((TOK, 1), f32), ((TOK, 1), f32), ((TOK, D), f32), ((BANDS * 8, 128), f32)]
    scratch = [pltpu.VMEM((len(blocks) * TOK, D), bf16)] * 2
    if final is None:
        out = tuple(sds(*s) for s in state_shape)
    else:
        args += final
        specs += [vmem] * len(final)
        out = sds((TOK, D), bf16)
        scratch += [pltpu.VMEM(*s) for s in state_shape]
    return call(
        functools.partial(attention_kernel, len(blocks), state is None, final is not None),
        out,
        *args,
        in_specs=specs,
        scratch=scratch,
        flops=len(blocks) * 1_200_000_000,
        name="attention",
    )


def mirrored(source, target, s):
    if (source // 4) % 2 == (target // 4) % 2:
        return s
    return (3 - s // 2) * 2 + s % 2


def later(distance):
    return [
        ((t - distance) * BANDS + mirrored(t - distance, t, s), t * BANDS + s)
        for t in range(distance, FRAMES)
        for s in range(BANDS)
    ]


def pointer_route(extra):
    pairs = []
    for t in range(FRAMES):
        for s in range(BANDS):
            source = t - (2 * s + extra)
            if source >= 0:
                pairs.append((source * BANDS + s, t * BANDS + s))
    return pairs


def over_space(x, target):
    return lax.ppermute(x, "space", [(i, target(i)) for i in range(BANDS)])


def sibling(i):
    return i ^ 1


def beside(i):
    return i ^ 2


def across(i):
    return (3 - i // 2) * 2 + i % 2


def body(
    features,
    masks,
    w_pix,
    mask_embed,
    w_conv,
    w_out,
    w_ptr,
    w_query,
    w_key,
    w_value,
    w_proj,
    mem_tpos,
    ptr_tpos,
    empty_memory,
):
    feat = features.reshape(TOK, D)
    joined, top, bottom, pooled = call(
        joined_kernel,
        (sds((TOK, D), bf16), sds((COLS, D), bf16), sds((COLS, D), bf16), sds((1, D), f32)),
        feat,
        masks.reshape(ROWS, COLS),
        w_pix,
        mask_embed.reshape(1, D),
        flops=70_000_000,
        name="joined",
    )
    above = lax.ppermute(bottom, "space", [(i, i + 1) for i in range(BANDS - 1)])
    below = lax.ppermute(top, "space", [(i + 1, i) for i in range(BANDS - 1)])
    pooled = pooled + over_space(pooled, sibling)
    pooled = pooled + over_space(pooled, beside)
    query = call(query_kernel, sds((TOK, D), bf16), feat, w_query, flops=70_000_000, name="query")
    memory, pairs = call(
        conv_kernel,
        (sds((ROWS, COLS * MEM), bf16), sds((HALF, 128), bf16)),
        joined,
        above,
        below,
        w_conv.reshape(3, 3 * D, D),
        w_out,
        scratch=[pltpu.VMEM(((ROWS + 2) * COLS, 3 * D), bf16), pltpu.VMEM((TOK, 128), f32)],
        flops=640_000_000,
        name="conv",
    )
    pointer = call(
        pointer_kernel,
        sds((1, D), bf16),
        pooled,
        over_space(pooled, across),
        w_ptr,
        flops=1_000_000,
        name="pointer",
    )
    near = lax.ppermute(pointer, BOTH, pointer_route(1))
    far = lax.ppermute(pointer, BOTH, pointer_route(2))
    earlier = [lax.ppermute(pairs, BOTH, later(d)) for d in range(1, MEMS + 1)]
    own = call(payload_kernel, sds((PAY, 128), bf16), *earlier, near, far, name="payload")

    here = lax.axis_index("space")
    holders = [here, beside(here), across(here), beside(across(here))]
    places = [jnp.stack([lax.axis_index("tm"), h, sibling(h)]).astype(jnp.int32) for h in holders]
    weights = (w_key, w_value, mem_tpos, empty_memory.reshape(1, MEM))

    one = over_space(own, beside)
    two = over_space(own, across)
    three = over_space(two, beside)
    arrivals = [own, one, two, three]
    siblings = [over_space(x, sibling) for x in arrivals]
    state = None
    for place, mine, theirs in zip(places[:3], arrivals, siblings):
        state = attend(place, query, weights, [mine, theirs], state)
    attended = attend(
        places[3],
        query,
        weights,
        [three, siblings[3]],
        state,
        [feat, w_proj, ptr_tpos.reshape(POINTERS * 2, 128)],
    )
    return (
        attended.reshape(1, ROWS, COLS, D),
        memory.reshape(1, ROWS, COLS * MEM),
        pointer,
    )


def solution(mesh):
    return jax.shard_map(
        body,
        mesh=mesh,
        in_specs=(
            P("tm", "space", None, None),
            P("tm", "space", None),
            P(),
            P(),
            P(),
            P(),
            P(),
            P(),
            P(),
            P(),
            P(),
            P(),
            P(),
            P(),
        ),
        out_specs=(P("tm", "space", None, None), P("tm", "space", None), P("tm", None)),
        check_vma=False,
    )
```

```python
import functools

import jax
import jax.numpy as jnp
from jax import lax
from jax.experimental import pallas as pl
from jax.experimental.pallas import tpu as pltpu
from jax.sharding import PartitionSpec as P

MEMS = 3
POINTERS = 16
FRAMES = 32
BANDS = 8
ROWS = 8
COLS = 64
TOK = ROWS * COLS
HALF = TOK // 2
D = 256
MEM = 64
PAY = MEMS * HALF
BOTH = ("tm", "space")
bf16 = jnp.bfloat16
f32 = jnp.float32
NT = (((1,), (1,)), ((), ()))


def call(
    kernel, out_shape, *args, scratch=(), in_specs=None, aliases=None, flops=0, limit=48, any_out=False, name=None
):
    vmem = pl.BlockSpec(memory_space=pltpu.VMEM)
    return pl.pallas_call(
        kernel,
        out_shape=out_shape,
        in_specs=[vmem] * len(args) if in_specs is None else in_specs,
        out_specs=jax.tree.map(
            lambda _: pl.BlockSpec(memory_space=pl.ANY) if any_out else vmem, out_shape
        ),
        scratch_shapes=list(scratch),
        input_output_aliases=aliases or {},
        compiler_params=pltpu.CompilerParams(vmem_limit_bytes=limit << 20),
        cost_estimate=pl.CostEstimate(flops=flops, bytes_accessed=1 << 20, transcendentals=0),
        name=name,
    )(*args)


def sds(shape, dtype):
    return jax.ShapeDtypeStruct(shape, dtype)


def fetch(pairs, sems):
    copies = [pltpu.make_async_copy(a, b, sems.at[i]) for i, (a, b) in enumerate(pairs)]
    for copy in copies:
        copy.start()
    return copies


def joined_kernel(*refs):
    sources, outputs, refs = refs[:5], refs[5:10], refs[10:]
    joined, top, bottom, pooled, query = outputs
    feat, w_pix, mask, embed, w_query, sems = refs
    copies = fetch(zip(sources, refs[:5]), sems)
    for copy in copies[:4]:
        copy.wait()
    columns = mask[...].astype(f32).T
    row = embed[...].reshape(1, D).astype(f32)
    total = jnp.zeros((8, D), f32)
    for r in range(ROWS):
        rows = feat[r * COLS : (r + 1) * COLS, :]
        column = columns[:, r : r + 1]
        value = jnp.dot(rows, w_pix[...], preferred_element_type=f32) + column * row
        value = value.astype(bf16)
        joined[r * COLS : (r + 1) * COLS, :] = value
        if r == 0:
            top[...] = value
        if r == ROWS - 1:
            bottom[...] = value
        picked = rows.astype(f32) * column
        for k in range(COLS // 8):
            total = total + picked[k * 8 : (k + 1) * 8, :]
    pooled[...] = jnp.sum(total, axis=0, keepdims=True)
    copies[4].wait()
    for r in range(0, TOK, 128):
        x = feat[r : r + 128, :].astype(f32)
        x = x - jnp.mean(x, axis=1, keepdims=True)
        x = x * lax.rsqrt(jnp.mean(x * x, axis=1, keepdims=True) + 1e-05)
        y = jnp.dot(x.astype(bf16), w_query[...], preferred_element_type=f32)
        query[r : r + 128, :] = (y * D ** (-0.5)).astype(bf16)


def conv_kernel(*refs):
    sources, (memory, pairs), refs = refs[:5], refs[5:7], refs[7:]
    joined, above, below, w_conv, w_out, wide, tokens, sems = refs
    near = fetch(zip(sources[:3], refs[:3]), sems)
    taps = [(sources[3].at[a], w_conv.at[a]) for a in range(3)]
    copies = fetch(taps + [(sources[4], w_out)], sems.at[pl.ds(3, 4)])
    for copy in near:
        copy.wait()
    side = lax.broadcasted_iota(jnp.int32, (COLS, D), 0)
    for r in range(ROWS + 2):
        if r == 0:
            row = above[...]
        elif r == ROWS + 1:
            row = below[...]
        else:
            row = joined[(r - 1) * COLS : r * COLS, :]
        value = row.astype(f32)
        left = jnp.where(side == 0, 0.0, pltpu.roll(value, 1, 0))
        right = jnp.where(side == COLS - 1, 0.0, pltpu.roll(value, COLS - 1, 0))
        here = slice(r * COLS, (r + 1) * COLS)
        wide[here, 0:D] = left.astype(bf16)
        wide[here, D : 2 * D] = row
        wide[here, 2 * D : 3 * D] = right.astype(bf16)
    for copy in copies:
        copy.wait()
    w_twice = jnp.concatenate([w_out[...], w_out[...]], axis=0)
    for part in range(4):
        start = part * 2 * COLS
        total = None
        for a in range(3):
            window = wide[start + a * COLS : start + a * COLS + 2 * COLS, :]
            term = jnp.dot(window, w_conv[a], preferred_element_type=f32)
            total = term if total is None else total + term
        hidden = 0.5 * total * (
            1.0 + jnp.tanh(0.7978845608028654 * (total + 0.044715 * (total * total * total)))
        )
        tokens[start : start + 2 * COLS, :] = lax.dot_general(
            hidden.astype(bf16), w_twice, NT, preferred_element_type=f32
        )
    lane = lax.broadcasted_iota(jnp.int32, (8, 128), 1)
    for k in range(COLS // 2):
        even = tokens[pl.ds(2 * k, ROWS, stride=COLS), :]
        odd = tokens[pl.ds(2 * k + 1, ROWS, stride=COLS), :]
        memory[:, k * 128 : (k + 1) * 128] = jnp.where(lane < MEM, even, odd).astype(bf16)
    lane = lax.broadcasted_iota(jnp.int32, (HALF, 128), 1)
    pairs[...] = jnp.where(lane < MEM, tokens[0:HALF, :], tokens[HALF:TOK, :]).astype(bf16)


def place_rows(pieces):
    row = lax.broadcasted_iota(jnp.int32, (16, 128), 0)
    out = jnp.zeros((16, 128), f32)
    for i, piece in enumerate(pieces):
        for half in range(2):
            out = jnp.where(row == 2 * i + half, piece[:, half * 128 : (half + 1) * 128], out)
    return out


def pair_kernel(mine, other, w_ptr, own, pointer, out):
    pooled = mine[...] + other[...]
    scale = lax.rsqrt(jnp.mean(pooled * pooled, axis=1, keepdims=True) + 1e-06)
    normed = jnp.broadcast_to(pooled * scale, (8, D)).astype(bf16)
    y = jnp.dot(normed, w_ptr[...], preferred_element_type=f32)[0:1, :].astype(bf16)
    pointer[...] = y
    out[0:HALF, :] = own[...]
    out[HALF : HALF + 16, :] = place_rows([y.astype(f32)]).astype(bf16)


def payload_kernel(couple, first, second, third, out, window):
    out[0:HALF, :] = first[...]
    out[HALF : 2 * HALF, :] = second[0:HALF, :]
    out[2 * HALF : 3 * HALF, :] = third[...]
    row = lax.broadcasted_iota(jnp.int32, (16, 128), 0)
    behind = second[HALF : HALF + 16, :].astype(f32)
    mine = couple[HALF : HALF + 16, :].astype(f32)
    behind = jnp.where((row == 2) | (row == 3), pltpu.roll(behind, 2, 0), 0.0)
    window[...] = (mine + behind).astype(bf16)


def twice(w):
    zero = jnp.zeros_like(w)
    return jnp.concatenate(
        [jnp.concatenate([w, zero], axis=1), jnp.concatenate([zero, w], axis=1)], axis=0
    )


QT = 256
HOLDERS = (0, 1, 2, 3, 6, 7, 4, 5)


def attention_kernel(count, first, last, *refs):
    refs = list(refs)
    query, w_key, w_value, mem_tpos, empty = refs[:5]
    refs = refs[5:]
    blocks, refs = refs[:count], refs[count:]
    if first:
        state_in = None
    else:
        state_in, refs = refs[:3], refs[3:]
    if last:
        tails, refs = refs[:BANDS], refs[BANDS:]
        feat, w_proj, ptr_tpos, attended, keys, values, shifts, top, norm, mixed, ptr_tok = refs
    else:
        top, norm, mixed, keys, values, shifts = refs
    frame = lax.axis_index("tm")
    wk = twice(w_key[...])
    wv = twice(w_value[...])
    padded = jnp.concatenate([mem_tpos[...], jnp.zeros((8 - MEMS, MEM), bf16)], axis=0)
    tpos_keys = jnp.dot(padded, w_key[...], preferred_element_type=f32)
    if first:
        token = jnp.broadcast_to(empty[...], (8, MEM))
        null_key = jnp.dot(token, w_key[...], preferred_element_type=f32).astype(bf16)
        null_value = jnp.dot(token, w_value[...], preferred_element_type=f32).astype(bf16)
        score = jnp.sum(
            query[...].astype(f32) * null_key[0:1, :].astype(f32), axis=1, keepdims=True
        )
        top[...] = score
        norm[...] = jnp.ones_like(score)
        mixed[...] = jnp.broadcast_to(null_value[0:1, :].astype(f32), (TOK, D))
    else:
        for source, target in zip(state_in, (top, norm, mixed)):
            target[...] = source[...]

    def update(rows, scores, value_rows):
        old = top[rows, :]
        new = jnp.maximum(old, jnp.max(scores, axis=1, keepdims=True))
        weights = jnp.exp(scores - new)
        fade = jnp.exp(old - new)
        norm[rows, :] = norm[rows, :] * fade + jnp.sum(weights, axis=1, keepdims=True)
        mixed[rows, :] = mixed[rows, :] * fade + jnp.dot(
            weights.astype(bf16), value_rows, preferred_element_type=f32
        )
        top[rows, :] = new

    tiles = [slice(q * QT, (q + 1) * QT) for q in range(TOK // QT)]
    shifts[...] = tpos_keys

    @pl.loop(0, jnp.minimum(frame, MEMS))
    def _(d):
        shift = shifts[pl.ds(d, 1), :]
        for b, block in enumerate(blocks):
            x = block[pl.ds(pl.multiple_of(d * HALF, HALF), HALF), :]
            base = b * TOK
            k = jnp.dot(x, wk, preferred_element_type=f32)
            v = jnp.dot(x, wv, preferred_element_type=f32).astype(bf16)
            keys[base : base + HALF, :] = (k[:, :D] + shift).astype(bf16)
            keys[base + HALF : base + TOK, :] = (k[:, D:] + shift).astype(bf16)
            values[base : base + HALF, :] = v[:, :D]
            values[base + HALF : base + TOK, :] = v[:, D:]
        found = [
            lax.dot_general(query[rows, :], keys[...], NT, preferred_element_type=f32)
            for rows in tiles
        ]
        for rows, scores in zip(tiles, found):
            update(rows, scores, values[...])

    if last:
        widened = jnp.dot(ptr_tpos[...], wk, preferred_element_type=f32)
        lane = lax.broadcasted_iota(jnp.int32, (1, POINTERS * 4), 1)
        here = lax.axis_index("space")
        for tail, holder in zip(tails, HOLDERS):
            at = pl.ds(pl.multiple_of((here ^ holder) * 8, 8), 8)
            ptr_tok[at, :] = tail[...].astype(f32)[0:8, :]
        rows = [(2 * (i // 4) + i % 2) * 8 + 2 * (i % 4 // 2) for i in range(POINTERS)]
        tok = jnp.concatenate([ptr_tok[r : r + 2, :] for r in rows], axis=0).astype(bf16)
        k = (jnp.dot(tok, wk, preferred_element_type=f32) + widened).astype(bf16)
        v = jnp.dot(tok, wv, preferred_element_type=f32).astype(bf16)
        valid = frame >= (lane % (POINTERS * 2)) // 2 + 1
        k = jnp.concatenate([k[:, :D], k[:, D:]], axis=0)
        v = jnp.concatenate([v[:, :D], v[:, D:]], axis=0)
        for rows in tiles:
            scores = lax.dot_general(query[rows, :], k, NT, preferred_element_type=f32)
            update(rows, jnp.where(valid, scores, -jnp.inf), v)
        for rows in tiles:
            final = (mixed[rows, :] / norm[rows, :]).astype(bf16)
            attended[rows, :] = (
                feat[rows, :].astype(f32)
                + jnp.dot(final, w_proj[...], preferred_element_type=f32)
            ).astype(bf16)


def order_kernel(value, earlier, out):
    pass


def after(value, earlier):
    return call(
        order_kernel,
        sds(value.shape, value.dtype),
        value,
        earlier,
        in_specs=[pl.BlockSpec(memory_space=pl.ANY)] * 2,
        aliases={0: 0},
        any_out=True,
        name="order",
    )


def attend(query, weights, blocks, state=None, final=None):
    vmem = pl.BlockSpec(memory_space=pltpu.VMEM)
    args = [query, *weights, *blocks]
    specs = [vmem] * len(args)
    if state is not None:
        args += list(state)
        specs += [vmem] * 3
    state_shape = [((TOK, 1), f32), ((TOK, 1), f32), ((TOK, D), f32)]
    scratch = [pltpu.VMEM((len(blocks) * TOK, D), bf16)] * 2 + [pltpu.VMEM((8, D), f32)]
    if final is None:
        out = tuple(sds(*s) for s in state_shape)
    else:
        args += final
        specs += [vmem] * len(final)
        out = sds((TOK, D), bf16)
        scratch += [pltpu.VMEM(*s) for s in state_shape] + [pltpu.VMEM((BANDS * 8, 128), f32)]
    return call(
        functools.partial(attention_kernel, len(blocks), state is None, final is not None),
        out,
        *args,
        in_specs=specs,
        scratch=scratch,
        flops=len(blocks) * 1_200_000_000,
        name="attention",
    )


def mirrored(source, target, s):
    if (source // 4) % 2 == (target // 4) % 2:
        return s
    return across(s)


def later(distance):
    return [
        ((t - distance) * BANDS + mirrored(t - distance, t, s), t * BANDS + s)
        for t in range(distance, FRAMES)
        for s in range(BANDS)
    ]


def pointer_distance(s):
    return 4 * (s // 2) + s % 2 + 1


def pointer_route():
    pairs = []
    for t in range(FRAMES):
        for s in range(BANDS):
            source = t - pointer_distance(s)
            if source >= 0:
                pairs.append((source * BANDS + s, t * BANDS + s))
    return pairs


def over_space(x, target):
    return lax.ppermute(x, "space", [(i, target(i)) for i in range(BANDS)])


def sibling(i):
    return i ^ 1


def beside(i):
    return i ^ 2


def opposite(i):
    return i ^ 4


def across(i):
    return i ^ 6


def body(
    features,
    masks,
    w_pix,
    mask_embed,
    w_conv,
    w_out,
    w_ptr,
    w_query,
    w_key,
    w_value,
    w_proj,
    mem_tpos,
    ptr_tpos,
    empty_memory,
):
    feat = features.reshape(TOK, D)
    far = pl.BlockSpec(memory_space=pl.ANY)
    vmem = pl.BlockSpec(memory_space=pltpu.VMEM)
    joined, top, bottom, pooled, query = call(
        joined_kernel,
        (
            sds((TOK, D), bf16),
            sds((COLS, D), bf16),
            sds((COLS, D), bf16),
            sds((1, D), f32),
            sds((TOK, D), bf16),
        ),
        feat,
        w_pix,
        masks.reshape(ROWS, COLS),
        mask_embed,
        w_query,
        in_specs=[far] * 5,
        scratch=[
            pltpu.VMEM((TOK, D), bf16),
            pltpu.VMEM((D, D), bf16),
            pltpu.VMEM((ROWS, COLS), jnp.int32),
            pltpu.VMEM((D,), bf16),
            pltpu.VMEM((D, D), bf16),
            pltpu.SemaphoreType.DMA((5,)),
        ],
        flops=140_000_000,
        limit=60,
        name="joined",
    )
    above = lax.ppermute(bottom, "space", [(i, i + 1) for i in range(BANDS - 1)])
    below = lax.ppermute(top, "space", [(i + 1, i) for i in range(BANDS - 1)])
    pooled = pooled + over_space(pooled, sibling)
    pooled = pooled + over_space(pooled, beside)
    above = after(above, pooled)
    memory, pairs = call(
        conv_kernel,
        (sds((ROWS, COLS * MEM), bf16), sds((HALF, 128), bf16)),
        joined,
        above,
        below,
        w_conv.reshape(3, 3 * D, D),
        w_out.T,
        in_specs=[far] * 5,
        scratch=[
            pltpu.VMEM((TOK, D), bf16),
            pltpu.VMEM((COLS, D), bf16),
            pltpu.VMEM((COLS, D), bf16),
            pltpu.VMEM((3, 3 * D, D), bf16),
            pltpu.VMEM((MEM, D), bf16),
            pltpu.VMEM(((ROWS + 2) * COLS, 3 * D), bf16),
            pltpu.VMEM((TOK, 128), f32),
            pltpu.SemaphoreType.DMA((7,)),
        ],
        flops=640_000_000,
        limit=60,
        name="conv",
    )
    first = lax.ppermute(pairs, BOTH, later(1))
    third = lax.ppermute(pairs, BOTH, later(3))
    pointer, couple = call(
        pair_kernel,
        (sds((1, D), bf16), sds((HALF + 16, 128), bf16)),
        pooled,
        over_space(pooled, opposite),
        w_ptr,
        pairs,
        flops=1_000_000,
        name="pair",
    )
    second = lax.ppermute(couple, BOTH, later(2))
    own, window = call(
        payload_kernel,
        (sds((PAY, 128), bf16), sds((16, 128), bf16)),
        couple,
        first,
        second,
        third,
        name="payload",
    )

    weights = (w_key, w_value, mem_tpos, empty_memory.reshape(1, MEM))

    one = over_space(own, beside)
    two = over_space(own, across)
    tail = lax.ppermute(window, BOTH, pointer_route())
    state = attend(query, weights, [own, over_space(own, sibling)])
    two = after(two, state[2])
    tail = after(tail, state[2])
    three = over_space(two, beside)
    tails = [tail, over_space(tail, beside), over_space(tail, across)]
    state = attend(query, weights, [one, over_space(one, sibling)], state)
    three = after(three, state[2])
    tails[2] = after(tails[2], state[2])
    tails.append(over_space(tails[2], beside))
    state = attend(query, weights, [two, over_space(two, sibling)], state)
    attended = attend(
        query,
        weights,
        [three, over_space(three, sibling)],
        state,
        [
            *(x for t in tails for x in (t, over_space(t, sibling))),
            feat,
            w_proj,
            ptr_tpos.reshape(POINTERS * 2, 128),
        ],
    )
    return (
        attended.reshape(1, ROWS, COLS, D),
        memory.reshape(1, ROWS, COLS * MEM),
        pointer,
    )


def solution(mesh):
    return jax.shard_map(
        body,
        mesh=mesh,
        in_specs=(
            P("tm", "space", None, None),
            P("tm", "space", None),
            P(),
            P(),
            P(),
            P(),
            P(),
            P(),
            P(),
            P(),
            P(),
            P(),
            P(),
            P(),
        ),
        out_specs=(P("tm", "space", None, None), P("tm", "space", None), P("tm", None)),
        check_vma=False,
    )
```

```python
import functools

import jax
import jax.numpy as jnp
from jax import lax
from jax.experimental import pallas as pl
from jax.experimental.pallas import tpu as pltpu
from jax.sharding import PartitionSpec as P

MEMS = 3
POINTERS = 16
FRAMES = 32
BANDS = 8
ROWS = 8
COLS = 64
TOK = ROWS * COLS
HALF = TOK // 2
D = 256
MEM = 64
PAY = MEMS * HALF
BOTH = ("tm", "space")
bf16 = jnp.bfloat16
f32 = jnp.float32
NT = (((1,), (1,)), ((), ()))


def call(
    kernel, out_shape, *args, scratch=(), in_specs=None, aliases=None, flops=0, limit=48, any_out=False, name=None
):
    vmem = pl.BlockSpec(memory_space=pltpu.VMEM)
    return pl.pallas_call(
        kernel,
        out_shape=out_shape,
        in_specs=[vmem] * len(args) if in_specs is None else in_specs,
        out_specs=jax.tree.map(
            lambda _: pl.BlockSpec(memory_space=pl.ANY) if any_out else vmem, out_shape
        ),
        scratch_shapes=list(scratch),
        input_output_aliases=aliases or {},
        compiler_params=pltpu.CompilerParams(vmem_limit_bytes=limit << 20),
        cost_estimate=pl.CostEstimate(flops=flops, bytes_accessed=1 << 20, transcendentals=0),
        name=name,
    )(*args)


def sds(shape, dtype):
    return jax.ShapeDtypeStruct(shape, dtype)


def fetch(pairs, sems):
    copies = [pltpu.make_async_copy(a, b, sems.at[i]) for i, (a, b) in enumerate(pairs)]
    for copy in copies:
        copy.start()
    return copies


def joined_kernel(*refs):
    sources, outputs, refs = refs[:5], refs[5:10], refs[10:]
    joined, outer, inner, pooled, query = outputs
    feat, w_pix, mask, embed, w_query, sems = refs
    copies = fetch(zip(sources, refs[:5]), sems)
    for copy in copies[:4]:
        copy.wait()
    columns = mask[...].astype(f32).T
    row = embed[...].reshape(1, D).astype(f32)
    total = jnp.zeros((8, D), f32)
    for r in range(ROWS):
        rows = feat[r * COLS : (r + 1) * COLS, :]
        column = columns[:, r : r + 1]
        value = jnp.dot(rows, w_pix[...], preferred_element_type=f32) + column * row
        value = value.astype(bf16)
        joined[r * COLS : (r + 1) * COLS, :] = value
        if r == 0:
            top = value
        picked = rows.astype(f32) * column
        for k in range(COLS // 8):
            total = total + picked[k * 8 : (k + 1) * 8, :]
    odd = lax.axis_index("space") % 2 == 1

    @pl.when(odd)
    def _():
        outer[...] = value
        inner[...] = top

    @pl.when(jnp.logical_not(odd))
    def _():
        outer[...] = top
        inner[...] = value

    pooled[...] = jnp.sum(total, axis=0, keepdims=True)
    copies[4].wait()
    for r in range(0, TOK, 128):
        x = feat[r : r + 128, :].astype(f32)
        x = x - jnp.mean(x, axis=1, keepdims=True)
        x = x * lax.rsqrt(jnp.mean(x * x, axis=1, keepdims=True) + 1e-05)
        y = jnp.dot(x.astype(bf16), w_query[...], preferred_element_type=f32)
        query[r : r + 128, :] = (y * D ** (-0.5)).astype(bf16)


def conv_kernel(*refs):
    sources, (memory, pairs), refs = refs[:5], refs[5:7], refs[7:]
    joined, outer, inner, w_conv, w_out, wide, tokens, sems = refs
    near = fetch(zip(sources[:3], refs[:3]), sems)
    taps = [(sources[3].at[a], w_conv.at[a]) for a in range(3)]
    copies = fetch(taps + [(sources[4], w_out)], sems.at[pl.ds(3, 4)])
    for copy in near:
        copy.wait()
    odd = lax.axis_index("space") % 2 == 1
    side = lax.broadcasted_iota(jnp.int32, (COLS, D), 0)
    for r in range(ROWS + 2):
        if r == 0:
            value = jnp.where(odd, inner[...].astype(f32), outer[...].astype(f32))
        elif r == ROWS + 1:
            value = jnp.where(odd, outer[...].astype(f32), inner[...].astype(f32))
        else:
            value = joined[(r - 1) * COLS : r * COLS, :].astype(f32)
        left = jnp.where(side == 0, 0.0, pltpu.roll(value, 1, 0))
        right = jnp.where(side == COLS - 1, 0.0, pltpu.roll(value, COLS - 1, 0))
        here = slice(r * COLS, (r + 1) * COLS)
        wide[here, 0:D] = left.astype(bf16)
        wide[here, D : 2 * D] = value.astype(bf16)
        wide[here, 2 * D : 3 * D] = right.astype(bf16)
    for copy in copies:
        copy.wait()
    w_twice = jnp.concatenate([w_out[...], w_out[...]], axis=0)
    for part in range(4):
        start = part * 2 * COLS
        total = None
        for a in range(3):
            window = wide[start + a * COLS : start + a * COLS + 2 * COLS, :]
            term = jnp.dot(window, w_conv[a], preferred_element_type=f32)
            total = term if total is None else total + term
        hidden = 0.5 * total * (
            1.0 + jnp.tanh(0.7978845608028654 * (total + 0.044715 * (total * total * total)))
        )
        tokens[start : start + 2 * COLS, :] = lax.dot_general(
            hidden.astype(bf16), w_twice, NT, preferred_element_type=f32
        )
    lane = lax.broadcasted_iota(jnp.int32, (8, 128), 1)
    for k in range(COLS // 2):
        even = tokens[pl.ds(2 * k, ROWS, stride=COLS), :]
        odd = tokens[pl.ds(2 * k + 1, ROWS, stride=COLS), :]
        memory[:, k * 128 : (k + 1) * 128] = jnp.where(lane < MEM, even, odd).astype(bf16)
    lane = lax.broadcasted_iota(jnp.int32, (HALF, 128), 1)
    pairs[...] = jnp.where(lane < MEM, tokens[0:HALF, :], tokens[HALF:TOK, :]).astype(bf16)


def place_rows(pieces):
    row = lax.broadcasted_iota(jnp.int32, (16, 128), 0)
    out = jnp.zeros((16, 128), f32)
    for i, piece in enumerate(pieces):
        for half in range(2):
            out = jnp.where(row == 2 * i + half, piece[:, half * 128 : (half + 1) * 128], out)
    return out


def pair_kernel(mine, other, w_ptr, own, pointer, out):
    pooled = mine[...] + other[...]
    scale = lax.rsqrt(jnp.mean(pooled * pooled, axis=1, keepdims=True) + 1e-06)
    normed = jnp.broadcast_to(pooled * scale, (8, D)).astype(bf16)
    y = jnp.dot(normed, w_ptr[...], preferred_element_type=f32)[0:1, :].astype(bf16)
    pointer[...] = y
    out[0:HALF, :] = own[...]
    out[HALF : HALF + 16, :] = place_rows([y.astype(f32)]).astype(bf16)


def payload_kernel(couple, first, second, third, out, window):
    out[0:HALF, :] = first[...]
    out[HALF : 2 * HALF, :] = second[0:HALF, :]
    out[2 * HALF : 3 * HALF, :] = third[...]
    row = lax.broadcasted_iota(jnp.int32, (16, 128), 0)
    behind = second[HALF : HALF + 16, :].astype(f32)
    mine = couple[HALF : HALF + 16, :].astype(f32)
    behind = jnp.where((row == 2) | (row == 3), pltpu.roll(behind, 2, 0), 0.0)
    window[...] = (mine + behind).astype(bf16)


def twice(w):
    zero = jnp.zeros_like(w)
    return jnp.concatenate(
        [jnp.concatenate([w, zero], axis=1), jnp.concatenate([zero, w], axis=1)], axis=0
    )


QT = 256
HOLDERS = (0, 1, 2, 3, 4, 5, 6, 7)


def attention_kernel(count, first, last, *refs):
    refs = list(refs)
    query, w_key, w_value, mem_tpos, empty = refs[:5]
    refs = refs[5:]
    blocks, refs = refs[:count], refs[count:]
    if first:
        state_in = None
    else:
        state_in, refs = refs[:3], refs[3:]
    if last:
        tails, refs = refs[:BANDS], refs[BANDS:]
        feat, w_proj, ptr_tpos, attended, keys, values, top, norm, mixed, ptr_tok = refs
    else:
        top, norm, mixed, keys, values = refs
    frame = lax.axis_index("tm")
    wk = twice(w_key[...])
    wv = twice(w_value[...])
    padded = jnp.concatenate([mem_tpos[...], jnp.zeros((8 - MEMS, MEM), bf16)], axis=0)
    tpos_keys = jnp.dot(padded, w_key[...], preferred_element_type=f32)
    if first:
        token = jnp.broadcast_to(empty[...], (8, MEM))
        null_key = jnp.dot(token, w_key[...], preferred_element_type=f32).astype(bf16)
        null_value = jnp.dot(token, w_value[...], preferred_element_type=f32).astype(bf16)
        score = jnp.sum(
            query[...].astype(f32) * null_key[0:1, :].astype(f32), axis=1, keepdims=True
        )
        top[...] = score
        norm[...] = jnp.ones_like(score)
        mixed[...] = jnp.broadcast_to(null_value[0:1, :].astype(f32), (TOK, D))
    else:
        for source, target in zip(state_in, (top, norm, mixed)):
            target[...] = source[...]

    def update(rows, scores, value_rows, valid=None):
        old = top[rows, :]
        new = jnp.maximum(old, jnp.max(scores, axis=1, keepdims=True))
        level = new
        if valid is not None:
            level = jnp.where(valid, new, jnp.inf)
            new = jnp.where(valid, new, old)
        weights = jnp.exp(scores - level)
        fade = jnp.exp(old - new)
        norm[rows, :] = norm[rows, :] * fade + jnp.sum(weights, axis=1, keepdims=True)
        mixed[rows, :] = mixed[rows, :] * fade + jnp.dot(
            weights.astype(bf16), value_rows, preferred_element_type=f32
        )
        top[rows, :] = new

    tiles = [slice(q * QT, (q + 1) * QT) for q in range(TOK // QT)]
    span = count * TOK
    for d in range(MEMS):
        shift = tpos_keys[d : d + 1, :]
        for b, block in enumerate(blocks):
            x = block[d * HALF : (d + 1) * HALF, :]
            base = d * span + b * TOK
            k = jnp.dot(x, wk, preferred_element_type=f32)
            v = jnp.dot(x, wv, preferred_element_type=f32).astype(bf16)
            keys[base : base + HALF, :] = (k[:, :D] + shift).astype(bf16)
            keys[base + HALF : base + TOK, :] = (k[:, D:] + shift).astype(bf16)
            values[base : base + HALF, :] = v[:, :D]
            values[base + HALF : base + TOK, :] = v[:, D:]

    def score(step):
        d, rows = step
        cols = slice(d * span, (d + 1) * span)
        return lax.dot_general(query[rows, :], keys[cols, :], NT, preferred_element_type=f32)

    steps = [(d, rows) for d in range(MEMS) for rows in tiles]
    coming = score(steps[0])
    for i, (d, rows) in enumerate(steps):
        scores = coming
        if i + 1 < len(steps):
            coming = score(steps[i + 1])
        update(rows, scores, values[d * span : (d + 1) * span, :], frame >= d + 1)

    if last:
        widened = jnp.dot(ptr_tpos[...], wk, preferred_element_type=f32)
        lane = lax.broadcasted_iota(jnp.int32, (1, POINTERS * 4), 1)
        here = lax.axis_index("space")
        for tail, holder in zip(tails, HOLDERS):
            at = pl.ds(pl.multiple_of((here ^ holder) * 8, 8), 8)
            ptr_tok[at, :] = tail[...].astype(f32)[0:8, :]
        rows = [(2 * (i // 4) + i % 2) * 8 + 2 * (i % 4 // 2) for i in range(POINTERS)]
        tok = jnp.concatenate([ptr_tok[r : r + 2, :] for r in rows], axis=0).astype(bf16)
        k = (jnp.dot(tok, wk, preferred_element_type=f32) + widened).astype(bf16)
        v = jnp.dot(tok, wv, preferred_element_type=f32).astype(bf16)
        valid = frame >= (lane % (POINTERS * 2)) // 2 + 1
        k = jnp.concatenate([k[:, :D], k[:, D:]], axis=0)
        v = jnp.concatenate([v[:, :D], v[:, D:]], axis=0)
        for rows in tiles:
            scores = lax.dot_general(query[rows, :], k, NT, preferred_element_type=f32)
            update(rows, jnp.where(valid, scores, -jnp.inf), v)
        for rows in tiles:
            final = (mixed[rows, :] / norm[rows, :]).astype(bf16)
            attended[rows, :] = (
                feat[rows, :].astype(f32)
                + jnp.dot(final, w_proj[...], preferred_element_type=f32)
            ).astype(bf16)


def order_kernel(value, earlier, out):
    pass


def after(value, earlier):
    return call(
        order_kernel,
        sds(value.shape, value.dtype),
        value,
        earlier,
        in_specs=[pl.BlockSpec(memory_space=pl.ANY)] * 2,
        aliases={0: 0},
        any_out=True,
        name="order",
    )


def attend(query, weights, blocks, state=None, final=None):
    vmem = pl.BlockSpec(memory_space=pltpu.VMEM)
    args = [query, *weights, *blocks]
    specs = [vmem] * len(args)
    if state is not None:
        args += list(state)
        specs += [vmem] * 3
    state_shape = [((TOK, 1), f32), ((TOK, 1), f32), ((TOK, D), f32)]
    scratch = [pltpu.VMEM((MEMS * len(blocks) * TOK, D), bf16)] * 2
    if final is None:
        out = tuple(sds(*s) for s in state_shape)
    else:
        args += final
        specs += [vmem] * len(final)
        out = sds((TOK, D), bf16)
        scratch += [pltpu.VMEM(*s) for s in state_shape] + [pltpu.VMEM((BANDS * 8, 128), f32)]
    return call(
        functools.partial(attention_kernel, len(blocks), state is None, final is not None),
        out,
        *args,
        in_specs=specs,
        scratch=scratch,
        flops=len(blocks) * 1_200_000_000,
        name="attention",
    )


def shifted(source, target, s):
    if (source // 4) % 2 == (target // 4) % 2:
        return s
    return opposite(s)


def later(distance):
    return [
        ((t - distance) * BANDS + shifted(t - distance, t, s), t * BANDS + s)
        for t in range(distance, FRAMES)
        for s in range(BANDS)
    ]


def pointer_distance(s):
    return 4 * (s // 2) + s % 2 + 1


def pointer_route():
    pairs = []
    for t in range(FRAMES):
        for s in range(BANDS):
            source = t - pointer_distance(s)
            if source >= 0:
                pairs.append((source * BANDS + shifted(source, t, s), t * BANDS + s))
    return pairs


def over_space(x, target):
    return lax.ppermute(x, "space", [(i, target(i)) for i in range(BANDS)])


def sibling(i):
    return i ^ 1


def beside(i):
    return i ^ 2


def opposite(i):
    return i ^ 4


def body(
    features,
    masks,
    w_pix,
    mask_embed,
    w_conv,
    w_out,
    w_ptr,
    w_query,
    w_key,
    w_value,
    w_proj,
    mem_tpos,
    ptr_tpos,
    empty_memory,
):
    feat = features.reshape(TOK, D)
    far = pl.BlockSpec(memory_space=pl.ANY)
    vmem = pl.BlockSpec(memory_space=pltpu.VMEM)
    joined, outer, inner, pooled, query = call(
        joined_kernel,
        (
            sds((TOK, D), bf16),
            sds((COLS, D), bf16),
            sds((COLS, D), bf16),
            sds((1, D), f32),
            sds((TOK, D), bf16),
        ),
        feat,
        w_pix,
        masks.reshape(ROWS, COLS),
        mask_embed,
        w_query,
        in_specs=[far] * 5,
        scratch=[
            pltpu.VMEM((TOK, D), bf16),
            pltpu.VMEM((D, D), bf16),
            pltpu.VMEM((ROWS, COLS), jnp.int32),
            pltpu.VMEM((D,), bf16),
            pltpu.VMEM((D, D), bf16),
            pltpu.SemaphoreType.DMA((5,)),
        ],
        flops=140_000_000,
        limit=60,
        name="joined",
    )
    links = [(i, i + 1) for i in range(1, BANDS - 1, 2)]
    outer = lax.ppermute(outer, "space", links + [(b, a) for a, b in links])
    inner = over_space(inner, sibling)
    pooled = pooled + over_space(pooled, sibling)
    pooled = pooled + over_space(pooled, beside)
    outer = after(outer, pooled)
    memory, pairs = call(
        conv_kernel,
        (sds((ROWS, COLS * MEM), bf16), sds((HALF, 128), bf16)),
        joined,
        outer,
        inner,
        w_conv.reshape(3, 3 * D, D),
        w_out.T,
        in_specs=[far] * 5,
        scratch=[
            pltpu.VMEM((TOK, D), bf16),
            pltpu.VMEM((COLS, D), bf16),
            pltpu.VMEM((COLS, D), bf16),
            pltpu.VMEM((3, 3 * D, D), bf16),
            pltpu.VMEM((MEM, D), bf16),
            pltpu.VMEM(((ROWS + 2) * COLS, 3 * D), bf16),
            pltpu.VMEM((TOK, 128), f32),
            pltpu.SemaphoreType.DMA((7,)),
        ],
        flops=640_000_000,
        limit=60,
        name="conv",
    )
    first = lax.ppermute(pairs, BOTH, later(1))
    third = lax.ppermute(pairs, BOTH, later(3))
    pointer, couple = call(
        pair_kernel,
        (sds((1, D), bf16), sds((HALF + 16, 128), bf16)),
        pooled,
        over_space(pooled, opposite),
        w_ptr,
        pairs,
        flops=1_000_000,
        name="pair",
    )
    second = lax.ppermute(couple, BOTH, later(2))
    own, window = call(
        payload_kernel,
        (sds((PAY, 128), bf16), sds((16, 128), bf16)),
        couple,
        first,
        second,
        third,
        name="payload",
    )

    weights = (w_key, w_value, mem_tpos, empty_memory.reshape(1, MEM))

    one = over_space(own, beside)
    two = over_space(own, opposite)
    tail = lax.ppermute(window, BOTH, pointer_route())
    state = attend(query, weights, [own, over_space(own, sibling)])
    two = after(two, state[2])
    tail = after(tail, state[2])
    three = over_space(two, beside)
    tails = [tail, over_space(tail, beside), over_space(tail, opposite)]
    state = attend(query, weights, [one, over_space(one, sibling)], state)
    three = after(three, state[2])
    tails[2] = after(tails[2], state[2])
    tails.append(over_space(tails[2], beside))
    state = attend(query, weights, [two, over_space(two, sibling)], state)
    attended = attend(
        query,
        weights,
        [three, over_space(three, sibling)],
        state,
        [
            *(x for t in tails for x in (t, over_space(t, sibling))),
            feat,
            w_proj,
            ptr_tpos.reshape(POINTERS * 2, 128),
        ],
    )
    return (
        attended.reshape(1, ROWS, COLS, D),
        memory.reshape(1, ROWS, COLS * MEM),
        pointer,
    )


def solution(mesh):
    return jax.shard_map(
        body,
        mesh=mesh,
        in_specs=(
            P("tm", "space", None, None),
            P("tm", "space", None),
            P(),
            P(),
            P(),
            P(),
            P(),
            P(),
            P(),
            P(),
            P(),
            P(),
            P(),
            P(),
        ),
        out_specs=(P("tm", "space", None, None), P("tm", "space", None), P("tm", None)),
        check_vma=False,
    )
```

```python
import functools

import jax
import jax.numpy as jnp
from jax import lax
from jax.experimental import pallas as pl
from jax.experimental.pallas import tpu as pltpu
from jax.sharding import PartitionSpec as P

MEMS = 3
POINTERS = 16
FRAMES = 32
BANDS = 8
ROWS = 8
COLS = 64
TOK = ROWS * COLS
HALF = TOK // 2
D = 256
MEM = 64
PAY = MEMS * HALF
BOTH = ("tm", "space")
bf16 = jnp.bfloat16
f32 = jnp.float32
NT = (((1,), (1,)), ((), ()))


def call(
    kernel, out_shape, *args, scratch=(), in_specs=None, aliases=None, flops=0, limit=48, any_out=False, name=None
):
    vmem = pl.BlockSpec(memory_space=pltpu.VMEM)
    return pl.pallas_call(
        kernel,
        out_shape=out_shape,
        in_specs=[vmem] * len(args) if in_specs is None else in_specs,
        out_specs=jax.tree.map(
            lambda _: pl.BlockSpec(memory_space=pl.ANY) if any_out else vmem, out_shape
        ),
        scratch_shapes=list(scratch),
        input_output_aliases=aliases or {},
        compiler_params=pltpu.CompilerParams(vmem_limit_bytes=limit << 20),
        cost_estimate=pl.CostEstimate(flops=flops, bytes_accessed=1 << 20, transcendentals=0),
        name=name,
    )(*args)


def sds(shape, dtype):
    return jax.ShapeDtypeStruct(shape, dtype)


def fetch(pairs, sems):
    copies = [pltpu.make_async_copy(a, b, sems.at[i]) for i, (a, b) in enumerate(pairs)]
    for copy in copies:
        copy.start()
    return copies


def joined_kernel(*refs):
    sources, outputs, refs = refs[:5], refs[5:10], refs[10:]
    joined, outer, inner, pooled, query = outputs
    feat, w_pix, mask, embed, w_query, sems = refs
    copies = fetch(zip(sources, refs[:5]), sems)
    for copy in copies[:4]:
        copy.wait()
    columns = mask[...].astype(f32).T
    row = embed[...].reshape(1, D).astype(f32)
    total = jnp.zeros((8, D), f32)
    for r in range(ROWS):
        rows = feat[r * COLS : (r + 1) * COLS, :]
        column = columns[:, r : r + 1]
        value = jnp.dot(rows, w_pix[...], preferred_element_type=f32) + column * row
        value = value.astype(bf16)
        joined[r * COLS : (r + 1) * COLS, :] = value
        if r == 0:
            top = value
        picked = rows.astype(f32) * column
        for k in range(COLS // 8):
            total = total + picked[k * 8 : (k + 1) * 8, :]
    odd = lax.axis_index("space") % 2 == 1

    @pl.when(odd)
    def _():
        outer[...] = value
        inner[...] = top

    @pl.when(jnp.logical_not(odd))
    def _():
        outer[...] = top
        inner[...] = value

    pooled[...] = jnp.sum(total, axis=0, keepdims=True)
    copies[4].wait()
    for r in range(0, TOK, 128):
        x = feat[r : r + 128, :].astype(f32)
        x = x - jnp.mean(x, axis=1, keepdims=True)
        x = x * lax.rsqrt(jnp.mean(x * x, axis=1, keepdims=True) + 1e-05)
        y = jnp.dot(x.astype(bf16), w_query[...], preferred_element_type=f32)
        query[r : r + 128, :] = (y * D ** (-0.5)).astype(bf16)


def conv_kernel(*refs):
    sources, (memory, pairs), refs = refs[:5], refs[5:7], refs[7:]
    joined, outer, inner, w_conv, w_out, wide, tokens, sems = refs
    near = fetch(zip(sources[:3], refs[:3]), sems)
    taps = [(sources[3].at[a], w_conv.at[a]) for a in range(3)]
    copies = fetch(taps + [(sources[4], w_out)], sems.at[pl.ds(3, 4)])
    for copy in near:
        copy.wait()
    odd = lax.axis_index("space") % 2 == 1
    side = lax.broadcasted_iota(jnp.int32, (COLS, D), 0)
    for r in range(ROWS + 2):
        if r == 0:
            value = jnp.where(odd, inner[...].astype(f32), outer[...].astype(f32))
        elif r == ROWS + 1:
            value = jnp.where(odd, outer[...].astype(f32), inner[...].astype(f32))
        else:
            value = joined[(r - 1) * COLS : r * COLS, :].astype(f32)
        left = jnp.where(side == 0, 0.0, pltpu.roll(value, 1, 0))
        right = jnp.where(side == COLS - 1, 0.0, pltpu.roll(value, COLS - 1, 0))
        here = slice(r * COLS, (r + 1) * COLS)
        wide[here, 0:D] = left.astype(bf16)
        wide[here, D : 2 * D] = value.astype(bf16)
        wide[here, 2 * D : 3 * D] = right.astype(bf16)
    for copy in copies:
        copy.wait()
    w_twice = jnp.concatenate([w_out[...], w_out[...]], axis=0)
    for part in range(4):
        start = part * 2 * COLS
        total = None
        for a in range(3):
            window = wide[start + a * COLS : start + a * COLS + 2 * COLS, :]
            term = jnp.dot(window, w_conv[a], preferred_element_type=f32)
            total = term if total is None else total + term
        hidden = 0.5 * total * (
            1.0 + jnp.tanh(0.7978845608028654 * (total + 0.044715 * (total * total * total)))
        )
        tokens[start : start + 2 * COLS, :] = lax.dot_general(
            hidden.astype(bf16), w_twice, NT, preferred_element_type=f32
        )
    lane = lax.broadcasted_iota(jnp.int32, (8, 128), 1)
    for k in range(COLS // 2):
        even = tokens[pl.ds(2 * k, ROWS, stride=COLS), :]
        odd = tokens[pl.ds(2 * k + 1, ROWS, stride=COLS), :]
        memory[:, k * 128 : (k + 1) * 128] = jnp.where(lane < MEM, even, odd).astype(bf16)
    lane = lax.broadcasted_iota(jnp.int32, (HALF, 128), 1)
    pairs[...] = jnp.where(lane < MEM, tokens[0:HALF, :], tokens[HALF:TOK, :]).astype(bf16)


def place_rows(pieces):
    row = lax.broadcasted_iota(jnp.int32, (16, 128), 0)
    out = jnp.zeros((16, 128), f32)
    for i, piece in enumerate(pieces):
        for half in range(2):
            out = jnp.where(row == 2 * i + half, piece[:, half * 128 : (half + 1) * 128], out)
    return out


def pair_kernel(mine, other, w_ptr, own, pointer, out):
    pooled = mine[...] + other[...]
    scale = lax.rsqrt(jnp.mean(pooled * pooled, axis=1, keepdims=True) + 1e-06)
    normed = jnp.broadcast_to(pooled * scale, (8, D)).astype(bf16)
    y = jnp.dot(normed, w_ptr[...], preferred_element_type=f32)[0:1, :].astype(bf16)
    pointer[...] = y
    out[0:HALF, :] = own[...]
    out[HALF : HALF + 16, :] = place_rows([y.astype(f32)]).astype(bf16)


def payload_kernel(couple, first, second, third, out, window):
    out[0:HALF, :] = first[...]
    out[HALF : 2 * HALF, :] = second[0:HALF, :]
    out[2 * HALF : 3 * HALF, :] = third[...]
    row = lax.broadcasted_iota(jnp.int32, (16, 128), 0)
    behind = second[HALF : HALF + 16, :].astype(f32)
    mine = couple[HALF : HALF + 16, :].astype(f32)
    behind = jnp.where((row == 2) | (row == 3), pltpu.roll(behind, 2, 0), 0.0)
    window[...] = (mine + behind).astype(bf16)


def join_kernel(block, tail, far, out):
    out[0:PAY, :] = block[...]
    out[PAY : PAY + 16, :] = tail[...]
    out[PAY + 16 : PAY + 32, :] = far[...]


def twice(w):
    zero = jnp.zeros_like(w)
    return jnp.concatenate(
        [jnp.concatenate([w, zero], axis=1), jnp.concatenate([zero, w], axis=1)], axis=0
    )


QT = 256


def attention_kernel(count, first, last, *refs):
    refs = list(refs)
    query, w_key, w_value, mem_tpos, empty = refs[:5]
    refs = refs[5:]
    blocks, refs = refs[:count], refs[count:]
    if first:
        state_in = None
    else:
        state_in, refs = refs[:3], refs[3:]
    if last:
        carriers, refs = refs[:2] + blocks, refs[2:]
        feat, w_proj, ptr_tpos, attended, keys, values, top, norm, mixed, ptr_tok = refs
    else:
        top, norm, mixed, keys, values = refs
    frame = lax.axis_index("tm")
    wk = twice(w_key[...])
    wv = twice(w_value[...])
    padded = jnp.concatenate([mem_tpos[...], jnp.zeros((8 - MEMS, MEM), bf16)], axis=0)
    tpos_keys = jnp.dot(padded, w_key[...], preferred_element_type=f32)
    if first:
        token = jnp.broadcast_to(empty[...], (8, MEM))
        null_key = jnp.dot(token, w_key[...], preferred_element_type=f32).astype(bf16)
        null_value = jnp.dot(token, w_value[...], preferred_element_type=f32).astype(bf16)
        score = jnp.sum(
            query[...].astype(f32) * null_key[0:1, :].astype(f32), axis=1, keepdims=True
        )
        top[...] = score
        norm[...] = jnp.ones_like(score)
        mixed[...] = jnp.broadcast_to(null_value[0:1, :].astype(f32), (TOK, D))
    else:
        for source, target in zip(state_in, (top, norm, mixed)):
            target[...] = source[...]

    def update(rows, scores, value_rows, valid=None):
        old = top[rows, :]
        new = jnp.maximum(old, jnp.max(scores, axis=1, keepdims=True))
        level = new
        if valid is not None:
            level = jnp.where(valid, new, jnp.inf)
            new = jnp.where(valid, new, old)
        weights = jnp.exp(scores - level)
        fade = jnp.exp(old - new)
        norm[rows, :] = norm[rows, :] * fade + jnp.sum(weights, axis=1, keepdims=True)
        mixed[rows, :] = mixed[rows, :] * fade + jnp.dot(
            weights.astype(bf16), value_rows, preferred_element_type=f32
        )
        top[rows, :] = new

    tiles = [slice(q * QT, (q + 1) * QT) for q in range(TOK // QT)]
    span = count * TOK
    for d in range(MEMS):
        shift = tpos_keys[d : d + 1, :]
        for b, block in enumerate(blocks):
            x = block[d * HALF : (d + 1) * HALF, :]
            base = d * span + b * TOK
            k = jnp.dot(x, wk, preferred_element_type=f32)
            v = jnp.dot(x, wv, preferred_element_type=f32).astype(bf16)
            keys[base : base + HALF, :] = (k[:, :D] + shift).astype(bf16)
            keys[base + HALF : base + TOK, :] = (k[:, D:] + shift).astype(bf16)
            values[base : base + HALF, :] = v[:, :D]
            values[base + HALF : base + TOK, :] = v[:, D:]

    def score(step):
        d, rows = step
        cols = slice(d * span, (d + 1) * span)
        return lax.dot_general(query[rows, :], keys[cols, :], NT, preferred_element_type=f32)

    steps = [(d, rows) for d in range(MEMS) for rows in tiles]
    coming = score(steps[0])
    for i, (d, rows) in enumerate(steps):
        scores = coming
        if i + 1 < len(steps):
            coming = score(steps[i + 1])
        update(rows, scores, values[d * span : (d + 1) * span, :], frame >= d + 1)

    if last:
        widened = jnp.dot(ptr_tpos[...], wk, preferred_element_type=f32)
        lane = lax.broadcasted_iota(jnp.int32, (1, POINTERS * 4), 1)
        here = lax.axis_index("space")
        for i, carrier in enumerate(carriers):
            for half in range(2):
                at = pl.ds(pl.multiple_of((here ^ (i + 4 * half)) * 8, 8), 8)
                start = PAY + 16 * half
                ptr_tok[at, :] = carrier[start : start + 16, :].astype(f32)[0:8, :]
        rows = [(2 * (i // 4) + i % 2) * 8 + 2 * (i % 4 // 2) for i in range(POINTERS)]
        tok = jnp.concatenate([ptr_tok[r : r + 2, :] for r in rows], axis=0).astype(bf16)
        k = (jnp.dot(tok, wk, preferred_element_type=f32) + widened).astype(bf16)
        v = jnp.dot(tok, wv, preferred_element_type=f32).astype(bf16)
        valid = frame >= (lane % (POINTERS * 2)) // 2 + 1
        k = jnp.concatenate([k[:, :D], k[:, D:]], axis=0)
        v = jnp.concatenate([v[:, :D], v[:, D:]], axis=0)
        for rows in tiles:
            scores = lax.dot_general(query[rows, :], k, NT, preferred_element_type=f32)
            update(rows, jnp.where(valid, scores, -jnp.inf), v)
        for rows in tiles:
            final = (mixed[rows, :] / norm[rows, :]).astype(bf16)
            attended[rows, :] = (
                feat[rows, :].astype(f32)
                + jnp.dot(final, w_proj[...], preferred_element_type=f32)
            ).astype(bf16)


def order_kernel(value, earlier, out):
    pass


def after(value, earlier):
    return call(
        order_kernel,
        sds(value.shape, value.dtype),
        value,
        earlier,
        in_specs=[pl.BlockSpec(memory_space=pl.ANY)] * 2,
        aliases={0: 0},
        any_out=True,
        name="order",
    )


def attend(query, weights, blocks, state=None, final=None):
    vmem = pl.BlockSpec(memory_space=pltpu.VMEM)
    args = [query, *weights, *blocks]
    specs = [vmem] * len(args)
    if state is not None:
        args += list(state)
        specs += [vmem] * 3
    state_shape = [((TOK, 1), f32), ((TOK, 1), f32), ((TOK, D), f32)]
    scratch = [pltpu.VMEM((MEMS * len(blocks) * TOK, D), bf16)] * 2
    if final is None:
        out = tuple(sds(*s) for s in state_shape)
    else:
        args += final
        specs += [vmem] * len(final)
        out = sds((TOK, D), bf16)
        scratch += [pltpu.VMEM(*s) for s in state_shape] + [pltpu.VMEM((BANDS * 8, 128), f32)]
    return call(
        functools.partial(attention_kernel, len(blocks), state is None, final is not None),
        out,
        *args,
        in_specs=specs,
        scratch=scratch,
        flops=len(blocks) * 1_200_000_000,
        name="attention",
    )


def shifted(source, target, s):
    if (source // 4) % 2 == (target // 4) % 2:
        return s
    return opposite(s)


def later(distance):
    return [
        ((t - distance) * BANDS + shifted(t - distance, t, s), t * BANDS + s)
        for t in range(distance, FRAMES)
        for s in range(BANDS)
    ]


def pointer_distance(s):
    return 4 * (s // 2) + s % 2 + 1


def pointer_route():
    pairs = []
    for t in range(FRAMES):
        for s in range(BANDS):
            source = t - pointer_distance(s)
            if source >= 0:
                pairs.append((source * BANDS + shifted(source, t, s), t * BANDS + s))
    return pairs


def over_space(x, target):
    return lax.ppermute(x, "space", [(i, target(i)) for i in range(BANDS)])


def sibling(i):
    return i ^ 1


def beside(i):
    return i ^ 2


def opposite(i):
    return i ^ 4


def body(
    features,
    masks,
    w_pix,
    mask_embed,
    w_conv,
    w_out,
    w_ptr,
    w_query,
    w_key,
    w_value,
    w_proj,
    mem_tpos,
    ptr_tpos,
    empty_memory,
):
    feat = features.reshape(TOK, D)
    far = pl.BlockSpec(memory_space=pl.ANY)
    vmem = pl.BlockSpec(memory_space=pltpu.VMEM)
    joined, outer, inner, pooled, query = call(
        joined_kernel,
        (
            sds((TOK, D), bf16),
            sds((COLS, D), bf16),
            sds((COLS, D), bf16),
            sds((1, D), f32),
            sds((TOK, D), bf16),
        ),
        feat,
        w_pix,
        masks.reshape(ROWS, COLS),
        mask_embed,
        w_query,
        in_specs=[far] * 5,
        scratch=[
            pltpu.VMEM((TOK, D), bf16),
            pltpu.VMEM((D, D), bf16),
            pltpu.VMEM((ROWS, COLS), jnp.int32),
            pltpu.VMEM((D,), bf16),
            pltpu.VMEM((D, D), bf16),
            pltpu.SemaphoreType.DMA((5,)),
        ],
        flops=140_000_000,
        limit=60,
        name="joined",
    )
    links = [(i, i + 1) for i in range(1, BANDS - 1, 2)]
    outer = lax.ppermute(outer, "space", links + [(b, a) for a, b in links])
    inner = over_space(inner, sibling)
    pooled = pooled + over_space(pooled, sibling)
    pooled = pooled + over_space(pooled, beside)
    outer = after(outer, pooled)
    memory, pairs = call(
        conv_kernel,
        (sds((ROWS, COLS * MEM), bf16), sds((HALF, 128), bf16)),
        joined,
        outer,
        inner,
        w_conv.reshape(3, 3 * D, D),
        w_out.T,
        in_specs=[far] * 5,
        scratch=[
            pltpu.VMEM((TOK, D), bf16),
            pltpu.VMEM((COLS, D), bf16),
            pltpu.VMEM((COLS, D), bf16),
            pltpu.VMEM((3, 3 * D, D), bf16),
            pltpu.VMEM((MEM, D), bf16),
            pltpu.VMEM(((ROWS + 2) * COLS, 3 * D), bf16),
            pltpu.VMEM((TOK, 128), f32),
            pltpu.SemaphoreType.DMA((7,)),
        ],
        flops=640_000_000,
        limit=60,
        name="conv",
    )
    first = lax.ppermute(pairs, BOTH, later(1))
    third = lax.ppermute(pairs, BOTH, later(3))
    pointer, couple = call(
        pair_kernel,
        (sds((1, D), bf16), sds((HALF + 16, 128), bf16)),
        pooled,
        over_space(pooled, opposite),
        w_ptr,
        pairs,
        flops=1_000_000,
        name="pair",
    )
    second = lax.ppermute(couple, BOTH, later(2))
    own, window = call(
        payload_kernel,
        (sds((PAY, 128), bf16), sds((16, 128), bf16)),
        couple,
        first,
        second,
        third,
        name="payload",
    )

    weights = (w_key, w_value, mem_tpos, empty_memory.reshape(1, MEM))

    one = over_space(own, beside)
    two = over_space(own, opposite)
    tail = lax.ppermute(window, BOTH, pointer_route())
    state = attend(query, weights, [own, over_space(own, sibling)])
    tail = after(tail, state[2])
    two = call(
        join_kernel,
        sds((PAY + 32, 128), bf16),
        two,
        tail,
        over_space(tail, opposite),
        name="join",
    )
    three = over_space(two, beside)
    state = attend(query, weights, [one, over_space(one, sibling)], state)
    two_beside = over_space(two, sibling)
    state = attend(query, weights, [two, two_beside], state)
    three = after(three, state[2])
    attended = attend(
        query,
        weights,
        [three, over_space(three, sibling)],
        state,
        [two, two_beside, feat, w_proj, ptr_tpos.reshape(POINTERS * 2, 128)],
    )
    return (
        attended.reshape(1, ROWS, COLS, D),
        memory.reshape(1, ROWS, COLS * MEM),
        pointer,
    )


def solution(mesh):
    return jax.shard_map(
        body,
        mesh=mesh,
        in_specs=(
            P("tm", "space", None, None),
            P("tm", "space", None),
            P(),
            P(),
            P(),
            P(),
            P(),
            P(),
            P(),
            P(),
            P(),
            P(),
            P(),
            P(),
        ),
        out_specs=(P("tm", "space", None, None), P("tm", "space", None), P("tm", None)),
        check_vma=False,
    )
```

```python
import functools

import jax
import jax.numpy as jnp
from jax import lax
from jax.experimental import pallas as pl
from jax.experimental.pallas import tpu as pltpu
from jax.sharding import PartitionSpec as P

MEMS = 3
POINTERS = 16
FRAMES = 32
BANDS = 8
ROWS = 8
COLS = 64
TOK = ROWS * COLS
HALF = TOK // 2
D = 256
MEM = 64
PAY = MEMS * HALF
BOTH = ("tm", "space")
bf16 = jnp.bfloat16
f32 = jnp.float32
NT = (((1,), (1,)), ((), ()))


def call(
    kernel, out_shape, *args, scratch=(), in_specs=None, aliases=None, flops=0, limit=48, any_out=False, name=None
):
    vmem = pl.BlockSpec(memory_space=pltpu.VMEM)
    return pl.pallas_call(
        kernel,
        out_shape=out_shape,
        in_specs=[vmem] * len(args) if in_specs is None else in_specs,
        out_specs=jax.tree.map(
            lambda _: pl.BlockSpec(memory_space=pl.ANY) if any_out else vmem, out_shape
        ),
        scratch_shapes=list(scratch),
        input_output_aliases=aliases or {},
        compiler_params=pltpu.CompilerParams(vmem_limit_bytes=limit << 20),
        cost_estimate=pl.CostEstimate(flops=flops, bytes_accessed=1 << 20, transcendentals=0),
        name=name,
    )(*args)


def sds(shape, dtype):
    return jax.ShapeDtypeStruct(shape, dtype)


def fetch(pairs, sems):
    copies = [pltpu.make_async_copy(a, b, sems.at[i]) for i, (a, b) in enumerate(pairs)]
    for copy in copies:
        copy.start()
    return copies


def joined_kernel(*refs):
    sources, outputs, refs = refs[:5], refs[5:10], refs[10:]
    joined, outer, inner, pooled, query = outputs
    feat, w_pix, mask, embed, w_query, sems = refs
    copies = fetch(zip(sources, refs[:5]), sems)
    for copy in copies[:4]:
        copy.wait()
    columns = mask[...].astype(f32).T
    row = embed[...].reshape(1, D).astype(f32)
    total = jnp.zeros((8, D), f32)
    for r in range(ROWS):
        rows = feat[r * COLS : (r + 1) * COLS, :]
        column = columns[:, r : r + 1]
        value = jnp.dot(rows, w_pix[...], preferred_element_type=f32) + column * row
        value = value.astype(bf16)
        joined[r * COLS : (r + 1) * COLS, :] = value
        if r == 0:
            top = value
        picked = rows.astype(f32) * column
        for k in range(COLS // 8):
            total = total + picked[k * 8 : (k + 1) * 8, :]
    odd = lax.axis_index("space") % 2 == 1

    @pl.when(odd)
    def _():
        outer[...] = value
        inner[...] = top

    @pl.when(jnp.logical_not(odd))
    def _():
        outer[...] = top
        inner[...] = value

    pooled[...] = jnp.sum(total, axis=0, keepdims=True)
    copies[4].wait()
    for r in range(0, TOK, 128):
        x = feat[r : r + 128, :].astype(f32)
        x = x - jnp.mean(x, axis=1, keepdims=True)
        x = x * lax.rsqrt(jnp.mean(x * x, axis=1, keepdims=True) + 1e-05)
        y = jnp.dot(x.astype(bf16), w_query[...], preferred_element_type=f32)
        query[r : r + 128, :] = (y * D ** (-0.5)).astype(bf16)


def conv_kernel(*refs):
    sources, (memory, pairs), refs = refs[:5], refs[5:7], refs[7:]
    joined, outer, inner, w_conv, w_out, wide, tokens, sems = refs
    near = fetch(zip(sources[:3], refs[:3]), sems)
    taps = [(sources[3].at[a], w_conv.at[a]) for a in range(3)]
    copies = fetch(taps + [(sources[4], w_out)], sems.at[pl.ds(3, 4)])
    for copy in near:
        copy.wait()
    odd = lax.axis_index("space") % 2 == 1
    side = lax.broadcasted_iota(jnp.int32, (COLS, D), 0)
    for r in range(ROWS + 2):
        if r == 0:
            value = jnp.where(odd, inner[...].astype(f32), outer[...].astype(f32))
        elif r == ROWS + 1:
            value = jnp.where(odd, outer[...].astype(f32), inner[...].astype(f32))
        else:
            value = joined[(r - 1) * COLS : r * COLS, :].astype(f32)
        left = jnp.where(side == 0, 0.0, pltpu.roll(value, 1, 0))
        right = jnp.where(side == COLS - 1, 0.0, pltpu.roll(value, COLS - 1, 0))
        here = slice(r * COLS, (r + 1) * COLS)
        wide[here, 0:D] = left.astype(bf16)
        wide[here, D : 2 * D] = value.astype(bf16)
        wide[here, 2 * D : 3 * D] = right.astype(bf16)
    for part in range(4):
        start = part * 2 * COLS
        total = None
        for a in range(3):
            if part == 0:
                copies[a].wait()
            window = wide[start + a * COLS : start + a * COLS + 2 * COLS, :]
            term = jnp.dot(window, w_conv[a], preferred_element_type=f32)
            total = term if total is None else total + term
        if part == 0:
            copies[3].wait()
            w_twice = jnp.concatenate([w_out[...], w_out[...]], axis=0)
        hidden = 0.5 * total * (
            1.0 + jnp.tanh(0.7978845608028654 * (total + 0.044715 * (total * total * total)))
        )
        tokens[start : start + 2 * COLS, :] = lax.dot_general(
            hidden.astype(bf16), w_twice, NT, preferred_element_type=f32
        )
    lane = lax.broadcasted_iota(jnp.int32, (8, 128), 1)
    for k in range(COLS // 2):
        even = tokens[pl.ds(2 * k, ROWS, stride=COLS), :]
        odd = tokens[pl.ds(2 * k + 1, ROWS, stride=COLS), :]
        memory[:, k * 128 : (k + 1) * 128] = jnp.where(lane < MEM, even, odd).astype(bf16)
    lane = lax.broadcasted_iota(jnp.int32, (HALF, 128), 1)
    pairs[...] = jnp.where(lane < MEM, tokens[0:HALF, :], tokens[HALF:TOK, :]).astype(bf16)


def place_rows(pieces):
    row = lax.broadcasted_iota(jnp.int32, (16, 128), 0)
    out = jnp.zeros((16, 128), f32)
    for i, piece in enumerate(pieces):
        for half in range(2):
            out = jnp.where(row == 2 * i + half, piece[:, half * 128 : (half + 1) * 128], out)
    return out


def pair_kernel(mine, other, w_ptr, own, pointer, out):
    pooled = mine[...] + other[...]
    scale = lax.rsqrt(jnp.mean(pooled * pooled, axis=1, keepdims=True) + 1e-06)
    normed = jnp.broadcast_to(pooled * scale, (8, D)).astype(bf16)
    y = jnp.dot(normed, w_ptr[...], preferred_element_type=f32)[0:1, :].astype(bf16)
    pointer[...] = y
    out[0:HALF, :] = own[...]
    out[HALF : HALF + 16, :] = place_rows([y.astype(f32)]).astype(bf16)


def payload_kernel(couple, first, second, third, out, window):
    out[0:HALF, :] = first[...]
    out[HALF : 2 * HALF, :] = second[0:HALF, :]
    out[2 * HALF : 3 * HALF, :] = third[...]
    row = lax.broadcasted_iota(jnp.int32, (16, 128), 0)
    behind = second[HALF : HALF + 16, :].astype(f32)
    mine = couple[HALF : HALF + 16, :].astype(f32)
    behind = jnp.where((row == 2) | (row == 3), pltpu.roll(behind, 2, 0), 0.0)
    window[...] = (mine + behind).astype(bf16)


def join_kernel(block, tail, far, out):
    out[0:PAY, :] = block[...]
    out[PAY : PAY + 16, :] = tail[...]
    out[PAY + 16 : PAY + 32, :] = far[...]


def twice(w):
    zero = jnp.zeros_like(w)
    return jnp.concatenate(
        [jnp.concatenate([w, zero], axis=1), jnp.concatenate([zero, w], axis=1)], axis=0
    )


QT = 256


def attention_kernel(count, first, last, *refs):
    refs = list(refs)
    query, w_key, w_value, mem_tpos, empty = refs[:5]
    refs = refs[5:]
    blocks, refs = refs[:count], refs[count:]
    if first:
        state_in = None
    else:
        state_in, refs = refs[:3], refs[3:]
    if last:
        carriers, refs = refs[:2] + blocks, refs[2:]
        feat, w_proj, ptr_tpos, attended, keys, values, top, norm, mixed, ptr_tok = refs
    else:
        top, norm, mixed, keys, values = refs
    frame = lax.axis_index("tm")
    wk = twice(w_key[...])
    wv = twice(w_value[...])
    padded = jnp.concatenate([mem_tpos[...], jnp.zeros((8 - MEMS, MEM), bf16)], axis=0)
    tpos_keys = jnp.dot(padded, w_key[...], preferred_element_type=f32)
    if first:
        token = jnp.broadcast_to(empty[...], (8, MEM))
        null_key = jnp.dot(token, w_key[...], preferred_element_type=f32).astype(bf16)
        null_value = jnp.dot(token, w_value[...], preferred_element_type=f32).astype(bf16)
        score = jnp.sum(
            query[...].astype(f32) * null_key[0:1, :].astype(f32), axis=1, keepdims=True
        )
        top[...] = score
        norm[...] = jnp.ones_like(score)
        mixed[...] = jnp.broadcast_to(null_value[0:1, :].astype(f32), (TOK, D))
    else:
        for source, target in zip(state_in, (top, norm, mixed)):
            target[...] = source[...]

    def update(rows, scores, value_rows, valid=None):
        old = top[rows, :]
        new = jnp.maximum(old, jnp.max(scores, axis=1, keepdims=True))
        level = new
        if valid is not None:
            level = jnp.where(valid, new, jnp.inf)
            new = jnp.where(valid, new, old)
        weights = jnp.exp(scores - level)
        fade = jnp.exp(old - new)
        norm[rows, :] = norm[rows, :] * fade + jnp.sum(weights, axis=1, keepdims=True)
        mixed[rows, :] = mixed[rows, :] * fade + jnp.dot(
            weights.astype(bf16), value_rows, preferred_element_type=f32
        )
        top[rows, :] = new

    tiles = [slice(q * QT, (q + 1) * QT) for q in range(TOK // QT)]
    span = count * TOK
    for d in range(MEMS):
        shift = tpos_keys[d : d + 1, :]
        for b, block in enumerate(blocks):
            x = block[d * HALF : (d + 1) * HALF, :]
            base = d * span + b * TOK
            k = jnp.dot(x, wk, preferred_element_type=f32)
            v = jnp.dot(x, wv, preferred_element_type=f32).astype(bf16)
            keys[base : base + HALF, :] = (k[:, :D] + shift).astype(bf16)
            keys[base + HALF : base + TOK, :] = (k[:, D:] + shift).astype(bf16)
            values[base : base + HALF, :] = v[:, :D]
            values[base + HALF : base + TOK, :] = v[:, D:]

    def score(step):
        d, rows = step
        cols = slice(d * span, (d + 1) * span)
        return lax.dot_general(query[rows, :], keys[cols, :], NT, preferred_element_type=f32)

    steps = [(d, rows) for d in range(MEMS) for rows in tiles]
    coming = score(steps[0])
    for i, (d, rows) in enumerate(steps):
        scores = coming
        if i + 1 < len(steps):
            coming = score(steps[i + 1])
        update(rows, scores, values[d * span : (d + 1) * span, :], frame >= d + 1)

    if last:
        widened = jnp.dot(ptr_tpos[...], wk, preferred_element_type=f32)
        lane = lax.broadcasted_iota(jnp.int32, (1, POINTERS * 4), 1)
        here = lax.axis_index("space")
        for i, carrier in enumerate(carriers):
            for half in range(2):
                at = pl.ds(pl.multiple_of((here ^ (i + 4 * half)) * 8, 8), 8)
                start = PAY + 16 * half
                ptr_tok[at, :] = carrier[start : start + 16, :].astype(f32)[0:8, :]
        rows = [(2 * (i // 4) + i % 2) * 8 + 2 * (i % 4 // 2) for i in range(POINTERS)]
        tok = jnp.concatenate([ptr_tok[r : r + 2, :] for r in rows], axis=0).astype(bf16)
        k = (jnp.dot(tok, wk, preferred_element_type=f32) + widened).astype(bf16)
        v = jnp.dot(tok, wv, preferred_element_type=f32).astype(bf16)
        valid = frame >= (lane % (POINTERS * 2)) // 2 + 1
        k = jnp.concatenate([k[:, :D], k[:, D:]], axis=0)
        v = jnp.concatenate([v[:, :D], v[:, D:]], axis=0)
        for rows in tiles:
            scores = lax.dot_general(query[rows, :], k, NT, preferred_element_type=f32)
            update(rows, jnp.where(valid, scores, -jnp.inf), v)
        for rows in tiles:
            final = (mixed[rows, :] / norm[rows, :]).astype(bf16)
            attended[rows, :] = (
                feat[rows, :].astype(f32)
                + jnp.dot(final, w_proj[...], preferred_element_type=f32)
            ).astype(bf16)


def order_kernel(value, earlier, out):
    pass


def after(value, earlier):
    return call(
        order_kernel,
        sds(value.shape, value.dtype),
        value,
        earlier,
        in_specs=[pl.BlockSpec(memory_space=pl.ANY)] * 2,
        aliases={0: 0},
        any_out=True,
        name="order",
    )


def attend(query, weights, blocks, state=None, final=None):
    vmem = pl.BlockSpec(memory_space=pltpu.VMEM)
    args = [query, *weights, *blocks]
    specs = [vmem] * len(args)
    if state is not None:
        args += list(state)
        specs += [vmem] * 3
    state_shape = [((TOK, 1), f32), ((TOK, 1), f32), ((TOK, D), f32)]
    scratch = [pltpu.VMEM((MEMS * len(blocks) * TOK, D), bf16)] * 2
    if final is None:
        out = tuple(sds(*s) for s in state_shape)
    else:
        args += final
        specs += [vmem] * len(final)
        out = sds((TOK, D), bf16)
        scratch += [pltpu.VMEM(*s) for s in state_shape] + [pltpu.VMEM((BANDS * 8, 128), f32)]
    return call(
        functools.partial(attention_kernel, len(blocks), state is None, final is not None),
        out,
        *args,
        in_specs=specs,
        scratch=scratch,
        flops=len(blocks) * 1_200_000_000,
        name="attention",
    )


def shifted(source, target, s):
    if (source // 4) % 2 == (target // 4) % 2:
        return s
    return opposite(s)


def later(distance):
    return [
        ((t - distance) * BANDS + shifted(t - distance, t, s), t * BANDS + s)
        for t in range(distance, FRAMES)
        for s in range(BANDS)
    ]


def pointer_distance(s):
    return 4 * (s // 2) + s % 2 + 1


def pointer_route():
    pairs = []
    for t in range(FRAMES):
        for s in range(BANDS):
            source = t - pointer_distance(s)
            if source >= 0:
                pairs.append((source * BANDS + shifted(source, t, s), t * BANDS + s))
    return pairs


def over_space(x, target):
    return lax.ppermute(x, "space", [(i, target(i)) for i in range(BANDS)])


def sibling(i):
    return i ^ 1


def beside(i):
    return i ^ 2


def opposite(i):
    return i ^ 4


def body(
    features,
    masks,
    w_pix,
    mask_embed,
    w_conv,
    w_out,
    w_ptr,
    w_query,
    w_key,
    w_value,
    w_proj,
    mem_tpos,
    ptr_tpos,
    empty_memory,
):
    feat = features.reshape(TOK, D)
    far = pl.BlockSpec(memory_space=pl.ANY)
    vmem = pl.BlockSpec(memory_space=pltpu.VMEM)
    joined, outer, inner, pooled, query = call(
        joined_kernel,
        (
            sds((TOK, D), bf16),
            sds((COLS, D), bf16),
            sds((COLS, D), bf16),
            sds((1, D), f32),
            sds((TOK, D), bf16),
        ),
        feat,
        w_pix,
        masks.reshape(ROWS, COLS),
        mask_embed,
        w_query,
        in_specs=[far] * 5,
        scratch=[
            pltpu.VMEM((TOK, D), bf16),
            pltpu.VMEM((D, D), bf16),
            pltpu.VMEM((ROWS, COLS), jnp.int32),
            pltpu.VMEM((D,), bf16),
            pltpu.VMEM((D, D), bf16),
            pltpu.SemaphoreType.DMA((5,)),
        ],
        flops=140_000_000,
        limit=60,
        name="joined",
    )
    links = [(i, i + 1) for i in range(1, BANDS - 1, 2)]
    outer = lax.ppermute(outer, "space", links + [(b, a) for a, b in links])
    inner = over_space(inner, sibling)
    pooled = pooled + over_space(pooled, sibling)
    pooled = pooled + over_space(pooled, beside)
    outer = after(outer, pooled)
    memory, pairs = call(
        conv_kernel,
        (sds((ROWS, COLS * MEM), bf16), sds((HALF, 128), bf16)),
        joined,
        outer,
        inner,
        w_conv.reshape(3, 3 * D, D),
        w_out.T,
        in_specs=[far] * 5,
        scratch=[
            pltpu.VMEM((TOK, D), bf16),
            pltpu.VMEM((COLS, D), bf16),
            pltpu.VMEM((COLS, D), bf16),
            pltpu.VMEM((3, 3 * D, D), bf16),
            pltpu.VMEM((MEM, D), bf16),
            pltpu.VMEM(((ROWS + 2) * COLS, 3 * D), bf16),
            pltpu.VMEM((TOK, 128), f32),
            pltpu.SemaphoreType.DMA((7,)),
        ],
        flops=640_000_000,
        limit=60,
        name="conv",
    )
    first = lax.ppermute(pairs, BOTH, later(1))
    third = lax.ppermute(pairs, BOTH, later(3))
    pointer, couple = call(
        pair_kernel,
        (sds((1, D), bf16), sds((HALF + 16, 128), bf16)),
        pooled,
        over_space(pooled, opposite),
        w_ptr,
        pairs,
        flops=1_000_000,
        name="pair",
    )
    second = lax.ppermute(couple, BOTH, later(2))
    own, window = call(
        payload_kernel,
        (sds((PAY, 128), bf16), sds((16, 128), bf16)),
        couple,
        first,
        second,
        third,
        name="payload",
    )

    weights = (w_key, w_value, mem_tpos, empty_memory.reshape(1, MEM))

    one = over_space(own, beside)
    two = over_space(own, opposite)
    tail = lax.ppermute(window, BOTH, pointer_route())
    state = attend(query, weights, [own, over_space(own, sibling)])
    tail = after(tail, state[2])
    two = call(
        join_kernel,
        sds((PAY + 32, 128), bf16),
        two,
        tail,
        over_space(tail, opposite),
        name="join",
    )
    three = over_space(two, beside)
    state = attend(query, weights, [one, over_space(one, sibling)], state)
    two_beside = over_space(two, sibling)
    state = attend(query, weights, [two, two_beside], state)
    three = after(three, state[2])
    attended = attend(
        query,
        weights,
        [three, over_space(three, sibling)],
        state,
        [two, two_beside, feat, w_proj, ptr_tpos.reshape(POINTERS * 2, 128)],
    )
    return (
        attended.reshape(1, ROWS, COLS, D),
        memory.reshape(1, ROWS, COLS * MEM),
        pointer,
    )


def solution(mesh):
    return jax.shard_map(
        body,
        mesh=mesh,
        in_specs=(
            P("tm", "space", None, None),
            P("tm", "space", None),
            P(),
            P(),
            P(),
            P(),
            P(),
            P(),
            P(),
            P(),
            P(),
            P(),
            P(),
            P(),
        ),
        out_specs=(P("tm", "space", None, None), P("tm", "space", None), P("tm", None)),
        check_vma=False,
    )
```
